512 devices in a mesh: samples: 64 (over z, y), variants: 8 (over x, core).
Axes of the slice: x: 4, y: 4, z: 16, core: 2. Of those that a mesh axis runs over, the one named last changes fastest.
Arguments:
- genotypes: bfloat16 [49152, 16384], P('samples', 'variants'), may hold values from -6 to 6
- basis_in: bfloat16 [49152, 256], P('samples'), may hold values from -0.02734375 to 0.02734375
Outputs:
- basis_out: float32 [49152, 256], P('samples')
- factor: float32 [256, 256], replicated
The draws below stay inside these ranges and needn't reach their ends.
All inputs are finite; a program needn't handle non-finite values.
Results may differ from the reference program's by a relative error of at most 0.0026.
Values may be sent and summed in bfloat16 or wider, within the bound.
A program may use at most 64 MiB of HBM per device.

```python
import jax
import jax.numpy as jnp
from jax import lax

K = 256
SAMPLES = 49152
VARIANTS = 16384


def block_levels(stream_key, extent, shards, low, high):
    gain = 1.0
    for axis_at, parts in shards:
        steps = jax.random.uniform(jax.random.fold_in(jax.random.fold_in(stream_key, 6), axis_at), (parts,), jnp.float32, low / len(shards), high / len(shards))
        gain = gain * jnp.repeat(jnp.exp(steps), extent[axis_at] // parts).reshape((-1,) + (1,) * (len(extent) - 1 - axis_at))
    return gain


def gaussian(rng, shape, spread, bound, cuts=(), kind=jnp.bfloat16):
    level = block_levels(rng, shape, cuts, -0.22, 0.18) if cuts else 1.0
    entries = jax.random.normal(rng, shape, jnp.float32) * spread * level
    return jnp.minimum(jnp.maximum(entries, -bound), bound).astype(kind)


def setup_inputs(seed: int = 0) -> dict:
    seeds = jax.random.split(jax.random.key(seed), 3)
    return {
        "genotypes": gaussian(seeds[0], (SAMPLES, VARIANTS), 1.0, 6.0, ((0, 64), (1, 8))),
        "basis_in": gaussian(seeds[1], (SAMPLES, K), SAMPLES ** -0.5, 0.02734375, ((0, 64),)),
    }


def reference(genotypes, basis_in):
    loadings = lax.dot_general(genotypes.astype(jnp.float32), basis_in.astype(jnp.float32), (((0,), (0,)), ((), ())), preferred_element_type=jnp.float32).astype(jnp.bfloat16)
    scores = jnp.dot(genotypes.astype(jnp.float32), loadings.astype(jnp.float32), preferred_element_type=jnp.float32) * (1.0 / VARIANTS ** 0.5)
    gram = jnp.dot(scores.T, scores, precision=lax.Precision.HIGHEST) / SAMPLES
    lower = jnp.linalg.cholesky(gram)
    basis_out = lax.linalg.triangular_solve(lower, scores.T, left_side=True, lower=True).T
    return (basis_out, lower.T)
```

```python
import functools

import jax
import jax.numpy as jnp
from jax import lax
from jax.experimental import pallas as pl
from jax.experimental.pallas import tpu as pltpu
from jax.sharding import PartitionSpec as P

MESH = pl.DeviceIdType.MESH
NZ, NY, NX, NC = 16, 4, 4, 2
NQ = 4
F32, BF16 = jnp.float32, jnp.bfloat16
SHIFT = 4096.0
LOG_SHIFT = 8.317766166719343


def encode(x):
    s = x * SHIFT
    s2 = s * s
    return (s2 * s2 * s).astype(BF16)


def decode(y):
    y = y.astype(F32)
    r = jnp.exp(jnp.log(jnp.abs(y)) * 0.2 - LOG_SHIFT)
    return jnp.where(y < 0, -r, r)


def dot(a, b, dims, **kw):
    return lax.dot_general(a, b, (dims, ((), ())), preferred_element_type=F32, **kw)


def comm_kernel(
    scale, total, g_hbm, b_ref, scores_ref, gram_ref,
    gbuf, tf, ysend, yrecv, sf, zsend, zrecv, lall,
    spart, crecv, xrecv, sall, gp, gcrecv, gxrecv, gx, gyrecv, gzall, gall,
    load_sem, ys, yr, zs, zr, ls, lr, us, ur, ps, pr,
):
    samp, var = lax.axis_index("samples"), lax.axis_index("variants")
    z, y = lax.div(samp, NY), lax.rem(samp, NY)
    x, c = lax.div(var, NC), lax.rem(var, NC)

    def dev(dz, dy, dx, dc):
        return (
            lax.rem(z + dz, NZ) * NY + lax.rem(y + dy, NY),
            lax.rem(x + dx, NX) * NC + lax.rem(c + dc, NC),
        )

    def start(src, dst, send, recv, to):
        pltpu.make_async_remote_copy(
            src_ref=src, dst_ref=dst, send_sem=send, recv_sem=recv,
            device_id=to, device_id_type=MESH,
        ).start()

    def wait(ref, sem):
        pltpu.make_async_copy(ref, ref, sem).wait()

    def rows(i, n):
        return pl.ds(pl.multiple_of(i * n, n), n)

    plane = [(dy, dx, dc) for dy in range(NY) for dx in range(NX) for dc in range(NC)][1:]
    partners = [(dz, 0, 0, 0) for dz in range(1, NZ)] + [(0,) + p for p in plane]

    cols = gbuf.shape[2]
    loads = [
        pltpu.make_async_copy(g_hbm.at[:, pl.ds(q * cols, cols)], gbuf.at[q], load_sem.at[q])
        for q in range(NQ)
    ]
    for load in loads:
        load.start()
    barrier = pltpu.get_barrier_semaphore()
    for p in partners:
        pl.semaphore_signal(barrier, inc=1, device_id=dev(*p), device_id_type=MESH)

    def term(q):
        loads[q].wait()
        t = dot(b_ref[...], gbuf[q], ((0,), (0,)))
        for i in range(NY):
            tf[q, i] = t[:, i * 128:(i + 1) * 128]

    def send_y(q):
        for dy in range(1, NY):
            to = lax.rem(y + dy, NY)
            ysend[q, dy - 1] = encode(tf[q, to])
            start(ysend.at[q, dy - 1], yrecv.at[q, dy - 1], ys.at[q], yr.at[q], dev(0, dy, 0, 0))

    term(0)
    pl.semaphore_wait(barrier, len(partners))
    send_y(0)
    for q in range(1, NQ):
        term(q)
        send_y(q)
    for q in range(NQ):
        wait(yrecv.at[q], yr.at[q])
        s = tf[q, y]
        for i in range(NY - 1):
            s = s + decode(yrecv[q, i])
        sf[q] = s
        zsend[q] = encode(s)
        for dz in range(1, NZ):
            to = lax.rem(z + dz, NZ)
            start(zsend.at[q, rows(to, 16)], zrecv.at[q, pl.ds((dz - 1) * 16, 16)], zs.at[q], zr.at[q], dev(dz, 0, 0, 0))
    for q in range(NQ):
        wait(zrecv.at[q], zr.at[q])
        s = sf[q, rows(z, 16)]
        for i in range(NZ - 1):
            s = s + decode(zrecv[q, i * 16:(i + 1) * 16])
        lall[q, y, rows(z, 16)] = s.astype(BF16)
        for dz in range(1, NZ):
            mine = lall.at[q, y, rows(z, 16)]
            start(mine, mine, ls.at[q], lr.at[q], dev(dz, 0, 0, 0))
    for q in range(NQ):
        wait(lall.at[q, y, pl.ds(0, 240)], lr.at[q])
        for dy in range(1, NY):
            mine = lall.at[q, y]
            start(mine, mine, us.at[q], ur.at[q], dev(0, dy, 0, 0))
    for q in range(NQ):
        wait(lall.at[q, pl.ds(0, 3)], ur.at[q])
        part = jnp.concatenate([lall[q, i] for i in range(NY)], axis=1)
        t = dot(gbuf[q], part, ((1,), (1,)))
        if q == 0:
            spart[...] = t
        else:
            spart[...] += t
    half, chunk = spart.shape[0] // NC, spart.shape[0] // (NC * NX)
    other = lax.rem(c + 1, NC)
    start(spart.at[rows(other, half)], crecv, ps.at[0], pr.at[0], dev(0, 0, 0, 1))
    wait(crecv, pr.at[0])
    crecv[...] = crecv[...] + spart[rows(c, half)]
    for dx in range(1, NX):
        to = lax.rem(x + dx, NX)
        start(crecv.at[rows(to, chunk)], xrecv.at[dx - 1], ps.at[1], pr.at[1], dev(0, 0, dx, 0))
    wait(xrecv, pr.at[1])
    r = (((crecv[rows(x, chunk)] + xrecv[0]) + xrecv[1]) + xrecv[2]) * scale
    mine = c * NX + x
    sall[rows(mine, chunk)] = r
    gp[...] = dot(r, r, ((0,), (0,)), precision=lax.Precision.HIGHEST) * (1.0 / total)
    start(gp.at[rows(other, 128)], gcrecv, ps.at[2], pr.at[2], dev(0, 0, 0, 1))
    wait(gcrecv, pr.at[2])
    gcrecv[...] = gcrecv[...] + gp[rows(c, 128)]
    for dx in range(1, NX):
        to = lax.rem(x + dx, NX)
        start(gcrecv.at[rows(to, 32)], gxrecv.at[dx - 1], ps.at[3], pr.at[3], dev(0, 0, dx, 0))
    for dx in range(1, NX):
        own = sall.at[rows(mine, chunk)]
        start(own, own, ps.at[4], pr.at[4], dev(0, 0, dx, 0))
    wait(gxrecv, pr.at[3])
    gx[...] = ((gcrecv[rows(x, 32)] + gxrecv[0]) + gxrecv[1]) + gxrecv[2]
    for dy in range(1, NY):
        to = lax.rem(y + dy, NY)
        start(gx.at[rows(to, 8)], gyrecv.at[dy - 1], ps.at[5], pr.at[5], dev(0, dy, 0, 0))
    wait(gyrecv, pr.at[5])
    gzall[z] = ((gx[rows(y, 8)] + gyrecv[0]) + gyrecv[1]) + gyrecv[2]
    for dz in range(1, NZ):
        start(gzall.at[z], gzall.at[z], ps.at[6], pr.at[6], dev(dz, 0, 0, 0))
    wait(sall.at[pl.ds(0, 3 * chunk)], pr.at[4])
    own = sall.at[rows(c, half)]
    start(own, own, ps.at[7], pr.at[7], dev(0, 0, 0, 1))
    wait(gzall.at[pl.ds(0, NZ - 1)], pr.at[6])
    s = gzall[0]
    for i in range(1, NZ):
        s = s + gzall[i]
    own = gall.at[rows((c * NX + x) * NY + y, 8)]
    own[...] = s
    for p in plane:
        start(own, own, ps.at[8], pr.at[8], dev(0, *p))
    wait(sall.at[pl.ds(0, half)], pr.at[7])
    scores_ref[...] = sall[...]
    wait(gall.at[pl.ds(0, 248)], pr.at[8])
    gram_ref[...] = gall[...]
    for q in range(NQ):
        wait(ysend.at[q], ys.at[q])
        wait(zrecv.at[q], zs.at[q])
        wait(zrecv.at[q], ls.at[q])
        wait(lall.at[q, pl.ds(0, 3)], us.at[q])
    wait(crecv, ps.at[0])
    wait(xrecv, ps.at[1])
    wait(gcrecv, ps.at[2])
    wait(gxrecv, ps.at[3])
    wait(sall.at[pl.ds(0, 3 * chunk)], ps.at[4])
    wait(gyrecv, ps.at[5])
    wait(gzall.at[pl.ds(0, NZ - 1)], ps.at[6])
    wait(sall.at[pl.ds(0, half)], ps.at[7])
    wait(gall.at[pl.ds(0, 248)], ps.at[8])


def scores_and_gram(genotypes, basis_in):
    n, v = genotypes.shape
    k = basis_in.shape[1]
    total_samples = n * lax.axis_size("samples")
    scale = 1.0 / (v * lax.axis_size("variants")) ** 0.5
    part = v // NQ
    chunk = n // (NC * NX)
    dma = pltpu.SemaphoreType.DMA
    vmem = pl.BlockSpec(memory_space=pltpu.VMEM)
    return pl.pallas_call(
        functools.partial(comm_kernel, scale, total_samples),
        out_shape=[jax.ShapeDtypeStruct((n, k), F32), jax.ShapeDtypeStruct((k, k), F32)],
        in_specs=[pl.BlockSpec(memory_space=pl.ANY), vmem],
        out_specs=[vmem, vmem],
        scratch_shapes=[
            pltpu.VMEM((NQ, n, part), BF16),
            pltpu.VMEM((NQ, NY, k, 128), F32),
            pltpu.VMEM((NQ, NY - 1, k, 128), BF16),
            pltpu.VMEM((NQ, NY - 1, k, 128), BF16),
            pltpu.VMEM((NQ, k, 128), F32),
            pltpu.VMEM((NQ, k, 128), BF16),
            pltpu.VMEM((NQ, (NZ - 1) * 16, 128), BF16),
            pltpu.VMEM((NQ, NY, k, 128), BF16),
            pltpu.VMEM((n, k), F32),
            pltpu.VMEM((n // NC, k), F32),
            pltpu.VMEM((NX - 1, chunk, k), F32),
            pltpu.VMEM((n, k), F32),
            pltpu.VMEM((k, k), F32),
            pltpu.VMEM((k // NC, k), F32),
            pltpu.VMEM((NX - 1, 32, k), F32),
            pltpu.VMEM((32, k), F32),
            pltpu.VMEM((NY - 1, 8, k), F32),
            pltpu.VMEM((NZ, 8, k), F32),
            pltpu.VMEM((k, k), F32),
            dma((NQ,)),
            dma((NQ,)), dma((NQ,)), dma((NQ,)), dma((NQ,)),
            dma((NQ,)), dma((NQ,)), dma((NQ,)), dma((NQ,)),
            dma((9,)), dma((9,)),
        ],
        compiler_params=pltpu.CompilerParams(
            collective_id=0, has_side_effects=True, vmem_limit_bytes=48 << 20
        ),
        cost_estimate=pl.CostEstimate(flops=4 * n * v * k, bytes_accessed=2 * n * v, transcendentals=0),
        name="scores_and_gram",
    )(genotypes, basis_in)


def local(genotypes, basis_in):
    scores, gram = scores_and_gram(genotypes, basis_in)
    lower = jnp.linalg.cholesky(gram)
    new_rows = lax.linalg.triangular_solve(lower, scores.T, left_side=True, lower=True).T
    return (new_rows, lower.T)


def solution(mesh):
    placed = (P("samples", "variants"), P("samples", None))
    return jax.shard_map(
        local, mesh=mesh, in_specs=placed, out_specs=(P("samples", None), P()), check_vma=False
    )
```

```python
import functools

import jax
import jax.numpy as jnp
from jax import lax
from jax.experimental import pallas as pl
from jax.experimental.pallas import tpu as pltpu
from jax.sharding import PartitionSpec as P

MESH = pl.DeviceIdType.MESH
NZ, NY, NX, NC = 16, 4, 4, 2
NQ = 4
F32, BF16 = jnp.float32, jnp.bfloat16
SHIFT = 4096.0
LOG_SHIFT = 8.317766166719343


def encode(x):
    s = x * SHIFT
    s2 = s * s
    return (s2 * s2 * s).astype(BF16)


def decode(y):
    y = y.astype(F32)
    r = jnp.exp(jnp.log(jnp.abs(y)) * 0.2 - LOG_SHIFT)
    return jnp.where(y < 0, -r, r)


def dot(a, b, dims, **kw):
    return lax.dot_general(a, b, (dims, ((), ())), preferred_element_type=F32, **kw)


def comm_kernel(
    scale, total, g_hbm, b_ref, scores_ref, gram_ref,
    gbuf, tf, ysend, yrecv, sf, zsend, zrecv, lall,
    spart, crecv, xrecv, sall, gp, gcrecv, gxrecv, gx, gyrecv, gzall, gall,
    load_sem, ys, yr, zs, zr, ls, lr, us, ur, ps, pr,
):
    samp, var = lax.axis_index("samples"), lax.axis_index("variants")
    z, y = lax.div(samp, NY), lax.rem(samp, NY)
    x, c = lax.div(var, NC), lax.rem(var, NC)

    def dev(dz, dy, dx, dc):
        return (
            lax.rem(z + dz, NZ) * NY + lax.rem(y + dy, NY),
            lax.rem(x + dx, NX) * NC + lax.rem(c + dc, NC),
        )

    def start(src, dst, send, recv, to):
        pltpu.make_async_remote_copy(
            src_ref=src, dst_ref=dst, send_sem=send, recv_sem=recv,
            device_id=to, device_id_type=MESH,
        ).start()

    def wait(ref, sem):
        pltpu.make_async_copy(ref, ref, sem).wait()

    def rows(i, n):
        return pl.ds(pl.multiple_of(i * n, n), n)

    plane = [(dy, dx, dc) for dy in range(NY) for dx in range(NX) for dc in range(NC)][1:]
    partners = [(dz, 0, 0, 0) for dz in range(1, NZ)] + [(0,) + p for p in plane]

    cols = gbuf.shape[2]
    loads = [
        pltpu.make_async_copy(g_hbm.at[:, pl.ds(q * cols, cols)], gbuf.at[q], load_sem.at[q])
        for q in range(NQ)
    ]
    for load in loads:
        load.start()
    barrier = pltpu.get_barrier_semaphore()
    for p in partners:
        pl.semaphore_signal(barrier, inc=1, device_id=dev(*p), device_id_type=MESH)

    def term(q):
        loads[q].wait()
        t = dot(b_ref[...], gbuf[q], ((0,), (0,)))
        for i in range(NY):
            tf[q, i] = t[:, i * 128:(i + 1) * 128]

    def send_y(q):
        for dy in range(1, NY):
            to = lax.rem(y + dy, NY)
            ysend[q, dy - 1] = encode(tf[q, to])
            start(ysend.at[q, dy - 1], yrecv.at[q, dy - 1], ys.at[q], yr.at[q], dev(0, dy, 0, 0))

    term(0)
    pl.semaphore_wait(barrier, len(partners))
    send_y(0)
    for q in range(1, NQ):
        term(q)
        send_y(q)
    for q in range(NQ):
        wait(yrecv.at[q], yr.at[q])
        s = tf[q, y]
        for i in range(NY - 1):
            s = s + decode(yrecv[q, i])
        sf[q] = s
        zsend[q] = encode(s)
        for dz in range(1, NZ):
            to = lax.rem(z + dz, NZ)
            start(zsend.at[q, rows(to, 16)], zrecv.at[q, pl.ds((dz - 1) * 16, 16)], zs.at[q], zr.at[q], dev(dz, 0, 0, 0))
    for q in range(NQ):
        wait(zrecv.at[q], zr.at[q])
        s = sf[q, rows(z, 16)]
        for i in range(NZ - 1):
            s = s + decode(zrecv[q, i * 16:(i + 1) * 16])
        lall[q, y, rows(z, 16)] = s.astype(BF16)
        for dz in range(1, NZ):
            mine = lall.at[q, y, rows(z, 16)]
            start(mine, mine, ls.at[q], lr.at[q], dev(dz, 0, 0, 0))
    for q in range(NQ):
        wait(lall.at[q, y, pl.ds(0, 240)], lr.at[q])
        for dy in range(1, NY):
            mine = lall.at[q, y]
            start(mine, mine, us.at[q], ur.at[q], dev(0, dy, 0, 0))
    for q in range(NQ):
        wait(lall.at[q, pl.ds(0, 3)], ur.at[q])
        part = jnp.concatenate([lall[q, i] for i in range(NY)], axis=1)
        t = dot(gbuf[q], part, ((1,), (1,)))
        if q == 0:
            spart[...] = t
        else:
            spart[...] += t
    half, chunk = spart.shape[0] // NC, spart.shape[0] // (NC * NX)
    other = lax.rem(c + 1, NC)
    start(spart.at[rows(other, half)], crecv, ps.at[0], pr.at[0], dev(0, 0, 0, 1))
    wait(crecv, pr.at[0])
    crecv[...] = crecv[...] + spart[rows(c, half)]
    for dx in range(1, NX):
        to = lax.rem(x + dx, NX)
        start(crecv.at[rows(to, chunk)], xrecv.at[dx - 1], ps.at[1], pr.at[1], dev(0, 0, dx, 0))
    wait(xrecv, pr.at[1])
    r = (((crecv[rows(x, chunk)] + xrecv[0]) + xrecv[1]) + xrecv[2]) * scale
    mine = c * NX + x
    sall[rows(mine, chunk)] = r
    gp[...] = dot(r, r, ((0,), (0,)), precision=lax.Precision.HIGHEST) * (1.0 / total)
    start(gp.at[rows(other, 128)], gcrecv, ps.at[2], pr.at[2], dev(0, 0, 0, 1))
    wait(gcrecv, pr.at[2])
    gcrecv[...] = gcrecv[...] + gp[rows(c, 128)]
    for dx in range(1, NX):
        to = lax.rem(x + dx, NX)
        start(gcrecv.at[rows(to, 32)], gxrecv.at[dx - 1], ps.at[3], pr.at[3], dev(0, 0, dx, 0))
    for dx in range(1, NX):
        own = sall.at[rows(mine, chunk)]
        start(own, own, ps.at[4], pr.at[4], dev(0, 0, dx, 0))
    wait(gxrecv, pr.at[3])
    gx[...] = ((gcrecv[rows(x, 32)] + gxrecv[0]) + gxrecv[1]) + gxrecv[2]
    for dy in range(1, NY):
        to = lax.rem(y + dy, NY)
        start(gx.at[rows(to, 8)], gyrecv.at[dy - 1], ps.at[5], pr.at[5], dev(0, dy, 0, 0))
    wait(gyrecv, pr.at[5])
    gzall[z] = ((gx[rows(y, 8)] + gyrecv[0]) + gyrecv[1]) + gyrecv[2]
    for dz in range(1, NZ):
        start(gzall.at[z], gzall.at[z], ps.at[6], pr.at[6], dev(dz, 0, 0, 0))
    wait(sall.at[pl.ds(0, 3 * chunk)], pr.at[4])
    own = sall.at[rows(c, half)]
    start(own, own, ps.at[7], pr.at[7], dev(0, 0, 0, 1))
    wait(gzall.at[pl.ds(0, NZ - 1)], pr.at[6])
    s = gzall[0]
    for i in range(1, NZ):
        s = s + gzall[i]
    own = gall.at[rows((c * NX + x) * NY + y, 8)]
    own[...] = s
    for p in plane:
        start(own, own, ps.at[8], pr.at[8], dev(0, *p))
    wait(sall.at[pl.ds(0, half)], pr.at[7])
    scores_ref[...] = sall[...]
    wait(gall.at[pl.ds(0, 248)], pr.at[8])
    gram_ref[...] = gall[...]
    for q in range(NQ):
        wait(ysend.at[q], ys.at[q])
        wait(zrecv.at[q], zs.at[q])
        wait(zrecv.at[q], ls.at[q])
        wait(lall.at[q, pl.ds(0, 3)], us.at[q])
    wait(crecv, ps.at[0])
    wait(xrecv, ps.at[1])
    wait(gcrecv, ps.at[2])
    wait(gxrecv, ps.at[3])
    wait(sall.at[pl.ds(0, 3 * chunk)], ps.at[4])
    wait(gyrecv, ps.at[5])
    wait(gzall.at[pl.ds(0, NZ - 1)], ps.at[6])
    wait(sall.at[pl.ds(0, half)], ps.at[7])
    wait(gall.at[pl.ds(0, 248)], ps.at[8])


def scores_and_gram(genotypes, basis_in):
    n, v = genotypes.shape
    k = basis_in.shape[1]
    total_samples = n * lax.axis_size("samples")
    scale = 1.0 / (v * lax.axis_size("variants")) ** 0.5
    part = v // NQ
    chunk = n // (NC * NX)
    dma = pltpu.SemaphoreType.DMA
    vmem = pl.BlockSpec(memory_space=pltpu.VMEM)
    return pl.pallas_call(
        functools.partial(comm_kernel, scale, total_samples),
        out_shape=[jax.ShapeDtypeStruct((n, k), F32), jax.ShapeDtypeStruct((k, k), F32)],
        in_specs=[pl.BlockSpec(memory_space=pl.ANY), vmem],
        out_specs=[vmem, vmem],
        scratch_shapes=[
            pltpu.VMEM((NQ, n, part), BF16),
            pltpu.VMEM((NQ, NY, k, 128), F32),
            pltpu.VMEM((NQ, NY - 1, k, 128), BF16),
            pltpu.VMEM((NQ, NY - 1, k, 128), BF16),
            pltpu.VMEM((NQ, k, 128), F32),
            pltpu.VMEM((NQ, k, 128), BF16),
            pltpu.VMEM((NQ, (NZ - 1) * 16, 128), BF16),
            pltpu.VMEM((NQ, NY, k, 128), BF16),
            pltpu.VMEM((n, k), F32),
            pltpu.VMEM((n // NC, k), F32),
            pltpu.VMEM((NX - 1, chunk, k), F32),
            pltpu.VMEM((n, k), F32),
            pltpu.VMEM((k, k), F32),
            pltpu.VMEM((k // NC, k), F32),
            pltpu.VMEM((NX - 1, 32, k), F32),
            pltpu.VMEM((32, k), F32),
            pltpu.VMEM((NY - 1, 8, k), F32),
            pltpu.VMEM((NZ, 8, k), F32),
            pltpu.VMEM((k, k), F32),
            dma((NQ,)),
            dma((NQ,)), dma((NQ,)), dma((NQ,)), dma((NQ,)),
            dma((NQ,)), dma((NQ,)), dma((NQ,)), dma((NQ,)),
            dma((9,)), dma((9,)),
        ],
        compiler_params=pltpu.CompilerParams(
            collective_id=0, has_side_effects=True, vmem_limit_bytes=60 << 20
        ),
        cost_estimate=pl.CostEstimate(flops=4 * n * v * k, bytes_accessed=2 * n * v, transcendentals=0),
        name="scores_and_gram",
    )(genotypes, basis_in)


def eliminate(m, n, panel):
    rid = lax.broadcasted_iota(jnp.int32, (8, 128), 0)
    g = [m[8*i:8*i+8] for i in range(n//8)]
    done = []
    for j0 in range(0, n, panel):
        lo = j0//8
        cols = [[jnp.broadcast_to(g[i][:, j0+k:j0+k+1], (8,128)) for i in range(lo, n//8)] for k in range(panel)]
        for k in range(panel):
            j = j0+k
            v, s = j//8, j%8
            ck = cols[k]
            d = ck[v-lo][s:s+1]
            inv = 1.0/d
            row = g[v][s:s+1]
            done.append(row*lax.rsqrt(d))
            if j == n-1: break
            keep = rid > s
            rs = jnp.broadcast_to(row*inv, (8,128))
            ups = [jnp.broadcast_to(cols[k2][v-lo][s:s+1]*inv, (8,128)) for k2 in range(k+1, panel)]
            for i in range(v, n//8):
                c = ck[i-lo]
                if i == v:
                    if s == 7: continue
                    c = jnp.where(keep, c, 0.0)
                g[i] = g[i] - c*rs
                for k2 in range(k+1, panel):
                    cols[k2][i-lo] = cols[k2][i-lo] - c*ups[k2-k-1]
    return jnp.concatenate(done, axis=0)


def chol_body(gram, aug, panel, nb=64):
    n = gram.shape[0]
    r, c = (lax.broadcasted_iota(jnp.int32, (n, n), a) for a in (0, 1))
    aug[:, :n] = gram
    aug[:, n:] = jnp.where(r == c, 1.0, 0.0)
    rb, cb = (lax.broadcasted_iota(jnp.int32, (nb, nb), a) for a in (0, 1))
    eye = jnp.where(rb == cb, 1.0, 0.0)
    for b in range(n//nb):
        lo, hi = b*nb, (b+1)*nb
        m = eliminate(jnp.concatenate([aug[lo:hi, lo:hi], eye], axis=1), nb, panel)
        v = jnp.where(rb >= cb, m[:, nb:], 0.0)
        u = jnp.where(rb <= cb, m[:, :nb], 0.0)
        rest = dot(v, aug[lo:hi, :], ((1,), (0,)), precision=lax.Precision.HIGHEST)
        aug[lo:hi, :] = rest
        aug[lo:hi, lo:hi] = u
        if hi < n:
            aug[hi:, :] = aug[hi:, :] - dot(rest[:, hi:n], rest, ((0,), (0,)), precision=lax.Precision.HIGHEST)


def factor_kernel(panel, gram, scores, basis, factor, aug):
    n = gram.shape[0]
    chol_body(gram[...], aug, panel)
    r, c = (lax.broadcasted_iota(jnp.int32, (n, n), a) for a in (0, 1))
    factor[...] = jnp.where(r <= c, aug[:, :n], 0.0)
    basis[...] = dot(scores[...], jnp.where(r >= c, aug[:, n:], 0.0), ((1,), (1,)), precision=lax.Precision.HIGHEST)


def factor_and_basis(gram, scores):
    k = gram.shape[0]
    vmem = pl.BlockSpec(memory_space=pltpu.VMEM)
    return pl.pallas_call(
        functools.partial(factor_kernel, 8),
        out_shape=[jax.ShapeDtypeStruct(scores.shape, F32), jax.ShapeDtypeStruct(gram.shape, F32)],
        in_specs=[vmem, vmem],
        out_specs=[vmem, vmem],
        scratch_shapes=[pltpu.VMEM((k, 2 * k), F32)],
        compiler_params=pltpu.CompilerParams(vmem_limit_bytes=40 << 20),
        name="factor_and_basis",
    )(gram, scores)


def local(genotypes, basis_in):
    scores, gram = scores_and_gram(genotypes, basis_in)
    return tuple(factor_and_basis(gram, scores))


def solution(mesh):
    placed = (P("samples", "variants"), P("samples", None))
    return jax.shard_map(
        local, mesh=mesh, in_specs=placed, out_specs=(P("samples", None), P()), check_vma=False
    )
```

```python
import functools

import jax
import jax.numpy as jnp
from jax import lax
from jax.experimental import pallas as pl
from jax.experimental.pallas import tpu as pltpu
from jax.sharding import PartitionSpec as P

MESH = pl.DeviceIdType.MESH
NZ, NY, NX, NC = 16, 4, 4, 2
NQ = 4
F32, BF16 = jnp.float32, jnp.bfloat16
SHIFT = 4096.0
LOG_SHIFT = 8.317766166719343
WIDE_SHIFT = 16384.0
LOG_WIDE_SHIFT = 9.704060527839234


def encode(x):
    s = x * SHIFT
    s2 = s * s
    return (s2 * s2 * s).astype(BF16)


def decode(y):
    y = y.astype(F32)
    r = jnp.exp(jnp.log(jnp.abs(y)) * 0.2 - LOG_SHIFT)
    return jnp.where(y < 0, -r, r)


def encode_wide(x):
    s = x * WIDE_SHIFT
    return (s * s * s).astype(BF16)


def decode_wide(y):
    y = y.astype(F32)
    r = jnp.exp(jnp.log(jnp.abs(y)) * (1.0 / 3.0) - LOG_WIDE_SHIFT)
    return jnp.where(y < 0, -r, r)


def hops(d, n):
    return min(d, n - d)


def dot(a, b, dims, **kw):
    return lax.dot_general(a, b, (dims, ((), ())), preferred_element_type=F32, **kw)


def comm_kernel(
    scale, total, g_hbm, b_hbm, scores_ref, gram_ref,
    bbuf, gbuf, tf, ysend, yrecv, sf, zsend, zrecv, lall,
    spart, crecv, xsend, xrecv, sall, gp, gprecv, gzall,
    load_sem, out_sem, ys, yr, zs, zr, ls, lr, us, ur, ps, pr,
):
    samp, var = lax.axis_index("samples"), lax.axis_index("variants")
    z, y = lax.div(samp, NY), lax.rem(samp, NY)
    x, c = lax.div(var, NC), lax.rem(var, NC)

    def dev(dz, dy, dx, dc):
        return (
            lax.rem(z + dz, NZ) * NY + lax.rem(y + dy, NY),
            lax.rem(x + dx, NX) * NC + lax.rem(c + dc, NC),
        )

    def start(src, dst, send, recv, to):
        pltpu.make_async_remote_copy(
            src_ref=src, dst_ref=dst, send_sem=send, recv_sem=recv,
            device_id=to, device_id_type=MESH,
        ).start()

    def wait(ref, sem):
        pltpu.make_async_copy(ref, ref, sem).wait()

    def rows(i, n):
        return pl.ds(pl.multiple_of(i * n, n), n)

    plane = [(dy, dx, dc) for dy in range(NY) for dx in range(NX) for dc in range(NC)][1:]
    plane.sort(key=lambda p: -hops(p[0], NY) - hops(p[1], NX))
    far = sorted(range(1, NZ), key=lambda d: -hops(d, NZ))
    partners = [(dz, 0, 0, 0) for dz in far] + [(0,) + p for p in plane]

    cols = gbuf.shape[2]
    loads = [
        pltpu.make_async_copy(g_hbm.at[:, pl.ds(q * cols, cols)], gbuf.at[q], load_sem.at[q])
        for q in range(NQ)
    ]
    load_b = pltpu.make_async_copy(b_hbm, bbuf, load_sem.at[NQ])
    load_b.start()
    for load in loads:
        load.start()
    barrier = pltpu.get_barrier_semaphore()
    for p in partners:
        pl.semaphore_signal(barrier, inc=1, device_id=dev(*p), device_id_type=MESH)

    def term(q):
        loads[q].wait()
        t = dot(bbuf[...], gbuf[q], ((0,), (0,)))
        for i in range(NY):
            tf[q, i] = t[:, i * 128:(i + 1) * 128]

    def send_y(q):
        for dy in range(1, NY):
            to = lax.rem(y + dy, NY)
            ysend[q, dy - 1] = encode(tf[q, to])
            start(ysend.at[q, dy - 1], yrecv.at[q, dy - 1], ys.at[q], yr.at[q], dev(0, dy, 0, 0))

    load_b.wait()
    term(0)
    pl.semaphore_wait(barrier, len(partners))
    send_y(0)
    for q in range(1, NQ):
        term(q)
        send_y(q)
    for q in range(NQ):
        wait(yrecv.at[q], yr.at[q])
        s = tf[q, y]
        for i in range(NY - 1):
            s = s + decode(yrecv[q, i])
        sf[q] = s
        zsend[q] = encode(s)
        for dz in far:
            to = lax.rem(z + dz, NZ)
            start(zsend.at[q, rows(to, 16)], zrecv.at[q, pl.ds((dz - 1) * 16, 16)], zs.at[q], zr.at[q], dev(dz, 0, 0, 0))
    for q in range(NQ):
        wait(zrecv.at[q], zr.at[q])
        s = sf[q, rows(z, 16)]
        for i in range(NZ - 1):
            s = s + decode(zrecv[q, i * 16:(i + 1) * 16])
        lall[q, y, rows(z, 16)] = s.astype(BF16)
        for dz in far:
            mine = lall.at[q, y, rows(z, 16)]
            start(mine, mine, ls.at[q], lr.at[q], dev(dz, 0, 0, 0))
    for q in range(NQ):
        wait(lall.at[q, y, pl.ds(0, 240)], lr.at[q])
        for dy in range(1, NY):
            mine = lall.at[q, y]
            start(mine, mine, us.at[q], ur.at[q], dev(0, dy, 0, 0))
    for q in range(NQ):
        wait(lall.at[q, pl.ds(0, 3)], ur.at[q])
        part = jnp.concatenate([lall[q, i] for i in range(NY)], axis=1)
        t = dot(gbuf[q], part, ((1,), (1,)))
        if q == 0:
            spart[...] = t
        else:
            spart[...] += t
    half, chunk = spart.shape[0] // NC, spart.shape[0] // (NC * NX)
    other = lax.rem(c + 1, NC)
    start(spart.at[rows(other, half)], crecv, ps.at[0], pr.at[0], dev(0, 0, 0, 1))
    wait(crecv, pr.at[0])
    crecv[...] = crecv[...] + spart[rows(c, half)]
    xsend[...] = encode_wide(crecv[...])
    for dx in (2, 1, 3):
        to = lax.rem(x + dx, NX)
        start(xsend.at[rows(to, chunk)], xrecv.at[dx - 1], ps.at[1], pr.at[1], dev(0, 0, dx, 0))
    wait(xrecv, pr.at[1])
    r = crecv[rows(x, chunk)]
    for i in range(NX - 1):
        r = r + decode_wide(xrecv[i])
    r = r * scale
    mine = c * NX + x
    sall[rows(mine, chunk)] = r
    gp[...] = dot(r, r, ((0,), (0,)), precision=lax.Precision.HIGHEST) * (1.0 / total)
    for i, (dy, dx, dc) in enumerate(plane):
        to = (lax.rem(c + dc, NC) * NX + lax.rem(x + dx, NX)) * NY + lax.rem(y + dy, NY)
        start(gp.at[rows(to, 8)], gprecv.at[i], ps.at[2], pr.at[2], dev(0, dy, dx, dc))
    for dx in (2, 1, 3):
        own = sall.at[rows(mine, chunk)]
        start(own, own, ps.at[4], pr.at[4], dev(0, 0, dx, 0))
    wait(gprecv, pr.at[2])
    spot = (c * NX + x) * NY + y
    s = gp[rows(spot, 8)]
    for i in range(len(plane)):
        s = s + gprecv[i]
    gzall[z] = s
    for dz in far:
        start(gzall.at[z], gzall.at[z], ps.at[6], pr.at[6], dev(dz, 0, 0, 0))
    wait(sall.at[pl.ds(0, 3 * chunk)], pr.at[4])
    own = sall.at[rows(c, half)]
    start(own, own, ps.at[7], pr.at[7], dev(0, 0, 0, 1))
    keep = pltpu.make_async_copy(own, scores_ref.at[rows(c, half)], out_sem.at[0])
    keep.start()
    wait(sall.at[pl.ds(0, half)], pr.at[7])
    own = sall.at[rows(other, half)]
    keep2 = pltpu.make_async_copy(own, scores_ref.at[rows(other, half)], out_sem.at[1])
    keep2.start()
    wait(gzall.at[pl.ds(0, NZ - 1)], pr.at[6])
    s = gzall[0]
    for i in range(1, NZ):
        s = s + gzall[i]
    own = gram_ref.at[rows(spot, 8)]
    own[...] = s
    for p in plane:
        start(own, own, ps.at[8], pr.at[8], dev(0, *p))
    keep.wait()
    keep2.wait()
    wait(gram_ref.at[pl.ds(0, 248)], pr.at[8])
    for q in range(NQ):
        wait(ysend.at[q], ys.at[q])
        wait(zrecv.at[q], zs.at[q])
        wait(zrecv.at[q], ls.at[q])
        wait(lall.at[q, pl.ds(0, 3)], us.at[q])
    wait(crecv, ps.at[0])
    wait(xrecv, ps.at[1])
    wait(gprecv, ps.at[2])
    wait(sall.at[pl.ds(0, 3 * chunk)], ps.at[4])
    wait(gzall.at[pl.ds(0, NZ - 1)], ps.at[6])
    wait(sall.at[pl.ds(0, half)], ps.at[7])
    wait(gram_ref.at[pl.ds(0, 248)], ps.at[8])


def scores_and_gram(genotypes, basis_in):
    n, v = genotypes.shape
    k = basis_in.shape[1]
    total_samples = n * lax.axis_size("samples")
    scale = 1.0 / (v * lax.axis_size("variants")) ** 0.5
    part = v // NQ
    chunk = n // (NC * NX)
    dma = pltpu.SemaphoreType.DMA
    vmem = pl.BlockSpec(memory_space=pltpu.VMEM)
    return pl.pallas_call(
        functools.partial(comm_kernel, scale, total_samples),
        out_shape=[jax.ShapeDtypeStruct((n, k), F32), jax.ShapeDtypeStruct((k, k), F32)],
        in_specs=[pl.BlockSpec(memory_space=pl.ANY)] * 2,
        out_specs=[pl.BlockSpec(memory_space=pl.ANY), vmem],
        scratch_shapes=[
            pltpu.VMEM((n, k), BF16),
            pltpu.VMEM((NQ, n, part), BF16),
            pltpu.VMEM((NQ, NY, k, 128), F32),
            pltpu.VMEM((NQ, NY - 1, k, 128), BF16),
            pltpu.VMEM((NQ, NY - 1, k, 128), BF16),
            pltpu.VMEM((NQ, k, 128), F32),
            pltpu.VMEM((NQ, k, 128), BF16),
            pltpu.VMEM((NQ, (NZ - 1) * 16, 128), BF16),
            pltpu.VMEM((NQ, NY, k, 128), BF16),
            pltpu.VMEM((n, k), F32),
            pltpu.VMEM((n // NC, k), F32),
            pltpu.VMEM((n // NC, k), BF16),
            pltpu.VMEM((NX - 1, chunk, k), BF16),
            pltpu.VMEM((n, k), F32),
            pltpu.VMEM((k, k), F32),
            pltpu.VMEM((NX * NY * NC - 1, 8, k), F32),
            pltpu.VMEM((NZ, 8, k), F32),
            dma((NQ + 1,)), dma((2,)),
            dma((NQ,)), dma((NQ,)), dma((NQ,)), dma((NQ,)),
            dma((NQ,)), dma((NQ,)), dma((NQ,)), dma((NQ,)),
            dma((9,)), dma((9,)),
        ],
        compiler_params=pltpu.CompilerParams(
            collective_id=0, has_side_effects=True, vmem_limit_bytes=24 << 20
        ),
        cost_estimate=pl.CostEstimate(flops=4 * n * v * k, bytes_accessed=2 * n * v, transcendentals=0),
        name="scores_and_gram",
    )(*(pltpu.with_memory_space_constraint(a, pltpu.HBM) for a in (genotypes, basis_in)))


def eliminate(a, panel):
    n = a.shape[0]
    row, col = (lax.broadcasted_iota(jnp.int32, (n, n), i) for i in (0, 1))
    eye = jnp.where(row == col, 1.0, 0.0)
    sub = lax.broadcasted_iota(jnp.int32, (8, n), 0)
    left = [a[8 * i:8 * i + 8] for i in range(n // 8)]
    right = [eye[8 * i:8 * i + 8] for i in range(n // 8)]
    upper, inverse = [], []
    for j0 in range(0, n, panel):
        lo = j0 // 8
        cols = [
            [jnp.broadcast_to(g[:, j0 + k:j0 + k + 1], (8, n)) for g in left[lo:]]
            for k in range(panel)
        ]
        for k in range(panel):
            j = j0 + k
            v, s = j // 8, j % 8
            pivot = cols[k][v - lo][s:s + 1]
            inv = 1.0 / pivot
            root = lax.rsqrt(pivot)
            ra, rb = left[v][s:s + 1], right[v][s:s + 1]
            upper.append(ra * root)
            inverse.append(rb * root)
            if j == n - 1:
                break
            sa = jnp.broadcast_to(ra * inv, (8, n))
            sb = jnp.broadcast_to(rb * inv, (8, n))
            sc = [jnp.broadcast_to(cols[m][v - lo][s:s + 1] * inv, (8, n)) for m in range(k + 1, panel)]
            for i in range(v if s < 7 else v + 1, n // 8):
                c = cols[k][i - lo]
                if i == v:
                    c = jnp.where(sub > s, c, 0.0)
                left[i] = left[i] - c * sa
                right[i] = right[i] - c * sb
                for m in range(k + 1, panel):
                    cols[m][i - lo] = cols[m][i - lo] - c * sc[m - k - 1]
    upper = jnp.where(row <= col, jnp.concatenate(upper, axis=0), 0.0)
    inverse = jnp.where(row >= col, jnp.concatenate(inverse, axis=0), 0.0)
    return upper, inverse


def split(a):
    high = a.astype(BF16)
    return high, (a - high.astype(F32)).astype(BF16)


def dot3(a, b, dims):
    (ah, al), (bh, bl) = split(a), split(b)
    return dot(ah, bh, dims) + (dot(ah, bl, dims) + dot(al, bh, dims))


def factor_kernel(panel, gram, scores_hbm, basis_hbm, factor, scores, basis, sems):
    n = gram.shape[0]
    h = n // 2
    load = pltpu.make_async_copy(scores_hbm, scores, sems.at[0])
    load.start()
    u11, v1 = eliminate(gram[:h, :h], panel)
    load.wait()
    u12 = dot(v1, gram[:h, h:], ((1,), (0,)), precision=lax.Precision.HIGHEST)
    a22 = gram[h:, h:] - dot(u12, u12, ((0,), (0,)), precision=lax.Precision.HIGHEST)
    first = dot3(scores[:, :h], v1, ((1,), (1,)))
    rest = scores[:, h:] - dot3(first, u12, ((1,), (0,)))
    u22, v2 = eliminate(a22, panel)
    basis[0] = first
    basis[1] = dot3(rest, v2, ((1,), (1,)))
    out1 = pltpu.make_async_copy(basis.at[0], basis_hbm.at[:, pl.ds(0, h)], sems.at[1])
    out1.start()
    out2 = pltpu.make_async_copy(basis.at[1], basis_hbm.at[:, pl.ds(h, h)], sems.at[2])
    out2.start()
    factor[:h, :h] = u11
    factor[:h, h:] = u12
    factor[h:, :h] = jnp.zeros((h, h), F32)
    factor[h:, h:] = u22
    out1.wait()
    out2.wait()


def factor_and_basis(gram, scores):
    n, k = scores.shape
    vmem, hbm = pl.BlockSpec(memory_space=pltpu.VMEM), pl.BlockSpec(memory_space=pltpu.HBM)
    return pl.pallas_call(
        functools.partial(factor_kernel, 8),
        out_shape=[jax.ShapeDtypeStruct(scores.shape, F32), jax.ShapeDtypeStruct(gram.shape, F32)],
        in_specs=[vmem, hbm],
        out_specs=[hbm, vmem],
        scratch_shapes=[
            pltpu.VMEM((n, k), F32),
            pltpu.VMEM((2, n, k // 2), F32),
            pltpu.SemaphoreType.DMA((3,)),
        ],
        compiler_params=pltpu.CompilerParams(vmem_limit_bytes=40 << 20),
        name="factor_and_basis",
    )(gram, scores)


def local(genotypes, basis_in):
    scores, gram = scores_and_gram(genotypes, basis_in)
    return tuple(factor_and_basis(gram, scores))


def solution(mesh):
    placed = (P("samples", "variants"), P("samples", None))
    return jax.shard_map(
        local, mesh=mesh, in_specs=placed, out_specs=(P("samples", None), P()), check_vma=False
    )
```

```python
import functools

import jax
import jax.numpy as jnp
from jax import lax
from jax.experimental import pallas as pl
from jax.experimental.pallas import tpu as pltpu
from jax.sharding import PartitionSpec as P

MESH = pl.DeviceIdType.MESH
NZ, NY, NX, NC = 16, 4, 4, 2
NQ = 4
F32, BF16 = jnp.float32, jnp.bfloat16
SHIFT = 4096.0
LOG_SHIFT = 8.317766166719343
WIDE_SHIFT = 16384.0
LOG_WIDE_SHIFT = 9.704060527839234


def encode(x):
    s = x * SHIFT
    s2 = s * s
    return (s2 * s2 * s).astype(BF16)


def decode(y):
    y = y.astype(F32)
    r = jnp.exp(jnp.log(jnp.abs(y)) * 0.2 - LOG_SHIFT)
    return jnp.where(y < 0, -r, r)


def encode_wide(x):
    s = x * WIDE_SHIFT
    return (s * s * s).astype(BF16)


def decode_wide(y):
    y = y.astype(F32)
    r = jnp.exp(jnp.log(jnp.abs(y)) * (1.0 / 3.0) - LOG_WIDE_SHIFT)
    return jnp.where(y < 0, -r, r)


def hops(d, n):
    return min(d, n - d)


def dot(a, b, dims, **kw):
    return lax.dot_general(a, b, (dims, ((), ())), preferred_element_type=F32, **kw)


def comm_kernel(
    scale, total, g_hbm, b_hbm, scores_ref, gram_ref,
    bbuf, gbuf, tf, ysend, yrecv, sf, zsend, zrecv, lall,
    spart, crecv, xsend, xrecv, sall, gp, gprecv, gzall,
    load_sem, out_sem, known, ys, yr, zs, zr, ls, lr, us, ur, cs, cr, xs, xr, ps, pr,
):
    samp, var = lax.axis_index("samples"), lax.axis_index("variants")
    z, y = lax.div(samp, NY), lax.rem(samp, NY)
    x, c = lax.div(var, NC), lax.rem(var, NC)
    odd = lax.rem(z, 2)

    def dev(dz, dy, dx, dc):
        return (
            lax.rem(z + dz, NZ) * NY + lax.rem(y + dy, NY),
            lax.rem(x + dx, NX) * NC + lax.rem(c + dc, NC),
        )

    def start(src, dst, send, recv, to):
        pltpu.make_async_remote_copy(
            src_ref=src, dst_ref=dst, send_sem=send, recv_sem=recv,
            device_id=to, device_id_type=MESH,
        ).start()

    def wait(ref, sem):
        pltpu.make_async_copy(ref, ref, sem).wait()

    def signal(sem, to):
        pl.semaphore_signal(sem, inc=1, device_id=to, device_id_type=MESH)

    def rows(i, n):
        return pl.ds(pl.multiple_of(i * n, n), n)

    plane = [(dy, dx, dc) for dy in range(NY) for dx in range(NX) for dc in range(NC)][1:]
    plane.sort(key=lambda p: -hops(p[0], NY) - hops(p[1], NX))
    far = sorted(range(1, NZ), key=lambda d: -hops(d, NZ))
    near = [(dz, 0, 0, 0) for dz in (2, 14, 1, 15)] + [(0, dy, 0, 0) for dy in (2, 1, 3)]
    near += [(0, 0, dx, 0) for dx in (2, 1, 3)] + [(0, 0, 0, 1)]
    units = [(q, h) for q in range(NQ) for h in range(2)]

    load_b = pltpu.make_async_copy(b_hbm, bbuf, load_sem.at[NQ])
    load_b.start()
    cols = gbuf.shape[2]
    loads = [
        pltpu.make_async_copy(g_hbm.at[:, pl.ds(q * cols, cols)], gbuf.at[q], load_sem.at[q])
        for q in range(NQ)
    ]
    for load in loads:
        load.start()
    barrier = pltpu.get_barrier_semaphore()
    for p in near:
        signal(barrier, dev(*p))

    def term(q):
        loads[q].wait()
        t = dot(bbuf[...], gbuf[q], ((0,), (0,)))
        for i in range(NY):
            tf[q, i] = t[:, i * 128:(i + 1) * 128]

    def send_y(q):
        for h in range(2):
            for dy in (2, 1, 3):
                to = lax.rem(y + dy, NY)
                ysend[q, h, dy - 1] = encode(tf[q, to, h * 128:(h + 1) * 128])
                start(ysend.at[q, h, dy - 1], yrecv.at[q, h, dy - 1], ys.at[q], yr.at[q, h], dev(0, dy, 0, 0))

    load_b.wait()
    term(0)
    pl.semaphore_wait(barrier, len(near))
    for dz in (2, 14):
        signal(known.at[0], dev(dz, 0, 0, 0))
    send_y(0)
    term(1)
    send_y(1)
    pl.semaphore_wait(known.at[0], 2)
    for dz in (4, 12):
        signal(known.at[1], dev(dz, 0, 0, 0))
    for q in range(2, NQ):
        term(q)
        send_y(q)
    pl.semaphore_wait(known.at[1], 2)
    for q, h in units:
        wait(yrecv.at[q, h], yr.at[q, h])
        s = tf[q, y, h * 128:(h + 1) * 128]
        for i in range(NY - 1):
            s = s + decode(yrecv[q, h, i])
        sf[q, h] = s
        zsend[q, h] = encode(s)
        par = lax.rem(z + h, 2)
        for i in (4, 3, 5, 2, 6, 1, 7, 0):
            def send_tile(i=i):
                d = 2 * i + par
                to = lax.rem(z + d, NZ)
                start(
                    zsend.at[q, h, rows(lax.div(to, 2), 16)], zrecv.at[q, rows(d - 1, 16)],
                    zs.at[q], zr.at[q], dev(d, 0, 0, 0),
                )
            if i:
                send_tile()
            else:
                pl.when(par == 1)(send_tile)
    tile = odd * 8 + lax.div(z, 2)
    for q in range(NQ):
        wait(zrecv.at[q], zr.at[q])
        s = sf[q, odd, rows(lax.div(z, 2), 16)]
        for i in range(NZ - 1):
            s = s + decode(zrecv[q, i * 16:(i + 1) * 16])
        lall[q, y, rows(tile, 16)] = s.astype(BF16)
        for dz in far:
            mine = lall.at[q, y, rows(tile, 16)]
            start(mine, mine, ls.at[q], lr.at[q, odd], dev(dz, 0, 0, 0))
    for q, h in units:
        @pl.when(odd == h)
        def _():
            wait(lall.at[q, y, pl.ds(0, 112)], lr.at[q, h])

        @pl.when(odd != h)
        def _():
            wait(lall.at[q, y, pl.ds(0, 128)], lr.at[q, h])

        for dy in (2, 1, 3):
            mine = lall.at[q, y, pl.ds(h * 128, 128)]
            start(mine, mine, us.at[q], ur.at[q, h], dev(0, dy, 0, 0))
    half, chunk = spart.shape[1] // NC, spart.shape[1] // (NC * NX)
    other = lax.rem(c + 1, NC)
    for q, h in units:
        wait(yrecv.at[q, h], ur.at[q, h])
        part = jnp.concatenate([lall[q, i, h * 128:(h + 1) * 128] for i in range(NY)], axis=1)
        t = dot(gbuf[q], part, ((1,), (1,)))
        if q == 0:
            spart[h] = t
        else:
            spart[h] += t
        if q == NQ - 1:
            start(spart.at[h, rows(other, half)], crecv.at[h], cs.at[h], cr.at[h], dev(0, 0, 0, 1))
    for h in range(2):
        wait(crecv.at[h], cr.at[h])
        crecv[h] = crecv[h] + spart[h, rows(c, half)]
        xsend[h] = encode_wide(crecv[h])
        for dx in (2, 1, 3):
            to = lax.rem(x + dx, NX)
            start(xsend.at[h, rows(to, chunk)], xrecv.at[h, dx - 1], xs.at[h], xr.at[h], dev(0, 0, dx, 0))
    mine = c * NX + x
    r = []
    for h in range(2):
        wait(xrecv.at[h], xr.at[h])
        s = crecv[h, rows(x, chunk)]
        for i in range(NX - 1):
            s = s + decode_wide(xrecv[h, i])
        r.append(s * scale)
    r = jnp.concatenate(r, axis=1)
    sall[rows(mine, chunk)] = r
    gp[...] = dot(r, r, ((0,), (0,)), precision=lax.Precision.HIGHEST) * (1.0 / total)
    for i, (dy, dx, dc) in enumerate(plane):
        to = (lax.rem(c + dc, NC) * NX + lax.rem(x + dx, NX)) * NY + lax.rem(y + dy, NY)
        start(gp.at[rows(to, 8)], gprecv.at[i], ps.at[2], pr.at[2], dev(0, dy, dx, dc))
    for dx in (2, 1, 3):
        own = sall.at[rows(mine, chunk)]
        start(own, own, ps.at[4], pr.at[4], dev(0, 0, dx, 0))
    wait(gprecv, pr.at[2])
    spot = (c * NX + x) * NY + y
    s = gp[rows(spot, 8)]
    for i in range(len(plane)):
        s = s + gprecv[i]
    gzall[z] = s
    for dz in far:
        start(gzall.at[z], gzall.at[z], ps.at[6], pr.at[6], dev(dz, 0, 0, 0))
    wait(sall.at[pl.ds(0, 3 * chunk)], pr.at[4])
    own = sall.at[rows(c, half)]
    start(own, own, ps.at[7], pr.at[7], dev(0, 0, 0, 1))
    keep = pltpu.make_async_copy(own, scores_ref.at[rows(c, half)], out_sem.at[0])
    keep.start()
    wait(sall.at[pl.ds(0, half)], pr.at[7])
    own = sall.at[rows(other, half)]
    keep2 = pltpu.make_async_copy(own, scores_ref.at[rows(other, half)], out_sem.at[1])
    keep2.start()
    wait(gzall.at[pl.ds(0, NZ - 1)], pr.at[6])
    s = gzall[0]
    for i in range(1, NZ):
        s = s + gzall[i]
    own = gram_ref.at[rows(spot, 8)]
    own[...] = s
    for p in plane:
        start(own, own, ps.at[8], pr.at[8], dev(0, *p))
    keep.wait()
    keep2.wait()
    wait(gram_ref.at[pl.ds(0, 248)], pr.at[8])
    for q in range(NQ):
        wait(ysend.at[q], ys.at[q])
        wait(zrecv.at[q], zs.at[q])
        wait(zrecv.at[q], ls.at[q])
        wait(lall.at[q, pl.ds(0, 3)], us.at[q])
    for h in range(2):
        wait(crecv.at[h], cs.at[h])
        wait(xrecv.at[h], xs.at[h])
    wait(gprecv, ps.at[2])
    wait(sall.at[pl.ds(0, 3 * chunk)], ps.at[4])
    wait(gzall.at[pl.ds(0, NZ - 1)], ps.at[6])
    wait(sall.at[pl.ds(0, half)], ps.at[7])
    wait(gram_ref.at[pl.ds(0, 248)], ps.at[8])


def scores_and_gram(genotypes, basis_in):
    n, v = genotypes.shape
    k = basis_in.shape[1]
    total_samples = n * lax.axis_size("samples")
    scale = 1.0 / (v * lax.axis_size("variants")) ** 0.5
    part = v // NQ
    chunk = n // (NC * NX)
    dma = pltpu.SemaphoreType.DMA
    vmem = pl.BlockSpec(memory_space=pltpu.VMEM)
    return pl.pallas_call(
        functools.partial(comm_kernel, scale, total_samples),
        out_shape=[jax.ShapeDtypeStruct((n, k), F32), jax.ShapeDtypeStruct((k, k), F32)],
        in_specs=[pl.BlockSpec(memory_space=pl.ANY)] * 2,
        out_specs=[pl.BlockSpec(memory_space=pl.ANY), vmem],
        scratch_shapes=[
            pltpu.VMEM((n, k), BF16),
            pltpu.VMEM((NQ, n, part), BF16),
            pltpu.VMEM((NQ, NY, k, 128), F32),
            pltpu.VMEM((NQ, 2, NY - 1, k // 2, 128), BF16),
            pltpu.VMEM((NQ, 2, NY - 1, k // 2, 128), BF16),
            pltpu.VMEM((NQ, 2, k // 2, 128), F32),
            pltpu.VMEM((NQ, 2, k // 2, 128), BF16),
            pltpu.VMEM((NQ, (NZ - 1) * 16, 128), BF16),
            pltpu.VMEM((NQ, NY, k, 128), BF16),
            pltpu.VMEM((2, n, k // 2), F32),
            pltpu.VMEM((2, n // NC, k // 2), F32),
            pltpu.VMEM((2, n // NC, k // 2), BF16),
            pltpu.VMEM((2, NX - 1, chunk, k // 2), BF16),
            pltpu.VMEM((n, k), F32),
            pltpu.VMEM((k, k), F32),
            pltpu.VMEM((NX * NY * NC - 1, 8, k), F32),
            pltpu.VMEM((NZ, 8, k), F32),
            dma((NQ + 1,)), dma((2,)), pltpu.SemaphoreType.REGULAR((2,)),
            dma((NQ,)), dma((NQ, 2)), dma((NQ,)), dma((NQ,)),
            dma((NQ,)), dma((NQ, 2)), dma((NQ,)), dma((NQ, 2)),
            dma((2,)), dma((2,)), dma((2,)), dma((2,)),
            dma((9,)), dma((9,)),
        ],
        compiler_params=pltpu.CompilerParams(
            collective_id=0, has_side_effects=True, vmem_limit_bytes=24 << 20
        ),
        cost_estimate=pl.CostEstimate(flops=4 * n * v * k, bytes_accessed=2 * n * v, transcendentals=0),
        name="scores_and_gram",
    )(*(pltpu.with_memory_space_constraint(a, pltpu.HBM) for a in (genotypes, basis_in)))


def eliminate(a, panel):
    n = a.shape[0]
    row, col = (lax.broadcasted_iota(jnp.int32, (n, n), i) for i in (0, 1))
    eye = jnp.where(row == col, 1.0, 0.0)
    sub = lax.broadcasted_iota(jnp.int32, (8, n), 0)
    left = [a[8 * i:8 * i + 8] for i in range(n // 8)]
    right = [eye[8 * i:8 * i + 8] for i in range(n // 8)]
    upper, inverse = [], []
    for j0 in range(0, n, panel):
        lo = j0 // 8
        cols = [
            [jnp.broadcast_to(g[:, j0 + k:j0 + k + 1], (8, n)) for g in left[lo:]]
            for k in range(panel)
        ]
        for k in range(panel):
            j = j0 + k
            v, s = j // 8, j % 8
            pivot = cols[k][v - lo][s:s + 1]
            inv = 1.0 / pivot
            root = lax.rsqrt(pivot)
            ra, rb = left[v][s:s + 1], right[v][s:s + 1]
            upper.append(ra * root)
            inverse.append(rb * root)
            if j == n - 1:
                break
            sa = jnp.broadcast_to(ra * inv, (8, n))
            sb = jnp.broadcast_to(rb * inv, (8, n))
            sc = [jnp.broadcast_to(cols[m][v - lo][s:s + 1] * inv, (8, n)) for m in range(k + 1, panel)]
            for i in range(v if s < 7 else v + 1, n // 8):
                c = cols[k][i - lo]
                if i == v:
                    c = jnp.where(sub > s, c, 0.0)
                left[i] = left[i] - c * sa
                right[i] = right[i] - c * sb
                for m in range(k + 1, panel):
                    cols[m][i - lo] = cols[m][i - lo] - c * sc[m - k - 1]
    upper = jnp.where(row <= col, jnp.concatenate(upper, axis=0), 0.0)
    inverse = jnp.where(row >= col, jnp.concatenate(inverse, axis=0), 0.0)
    return upper, inverse


def split(a):
    high = a.astype(BF16)
    return high, (a - high.astype(F32)).astype(BF16)


def dot3(a, b, dims):
    (ah, al), (bh, bl) = split(a), split(b)
    return dot(ah, bh, dims) + (dot(ah, bl, dims) + dot(al, bh, dims))


def factor_kernel(panel, gram, scores_hbm, basis_hbm, factor, scores, basis, sems):
    n = gram.shape[0]
    h = n // 2
    load = pltpu.make_async_copy(scores_hbm, scores, sems.at[0])
    load.start()
    u11, v1 = eliminate(gram[:h, :h], panel)
    load.wait()
    u12 = dot(v1, gram[:h, h:], ((1,), (0,)), precision=lax.Precision.HIGHEST)
    a22 = gram[h:, h:] - dot(u12, u12, ((0,), (0,)), precision=lax.Precision.HIGHEST)
    first = dot3(scores[:, :h], v1, ((1,), (1,)))
    rest = scores[:, h:] - dot3(first, u12, ((1,), (0,)))
    u22, v2 = eliminate(a22, panel)
    basis[0] = first
    basis[1] = dot3(rest, v2, ((1,), (1,)))
    out1 = pltpu.make_async_copy(basis.at[0], basis_hbm.at[:, pl.ds(0, h)], sems.at[1])
    out1.start()
    out2 = pltpu.make_async_copy(basis.at[1], basis_hbm.at[:, pl.ds(h, h)], sems.at[2])
    out2.start()
    factor[:h, :h] = u11
    factor[:h, h:] = u12
    factor[h:, :h] = jnp.zeros((h, h), F32)
    factor[h:, h:] = u22
    out1.wait()
    out2.wait()


def factor_and_basis(gram, scores):
    n, k = scores.shape
    vmem, hbm = pl.BlockSpec(memory_space=pltpu.VMEM), pl.BlockSpec(memory_space=pltpu.HBM)
    return pl.pallas_call(
        functools.partial(factor_kernel, 8),
        out_shape=[jax.ShapeDtypeStruct(scores.shape, F32), jax.ShapeDtypeStruct(gram.shape, F32)],
        in_specs=[vmem, hbm],
        out_specs=[hbm, vmem],
        scratch_shapes=[
            pltpu.VMEM((n, k), F32),
            pltpu.VMEM((2, n, k // 2), F32),
            pltpu.SemaphoreType.DMA((3,)),
        ],
        compiler_params=pltpu.CompilerParams(vmem_limit_bytes=40 << 20),
        name="factor_and_basis",
    )(gram, scores)


def local(genotypes, basis_in):
    scores, gram = scores_and_gram(genotypes, basis_in)
    return tuple(factor_and_basis(gram, scores))


def solution(mesh):
    placed = (P("samples", "variants"), P("samples", None))
    return jax.shard_map(
        local, mesh=mesh, in_specs=placed, out_specs=(P("samples", None), P()), check_vma=False
    )
```

```python
import functools

import jax
import jax.numpy as jnp
from jax import lax
from jax.experimental import pallas as pl
from jax.experimental.pallas import tpu as pltpu
from jax.sharding import PartitionSpec as P

MESH = pl.DeviceIdType.MESH
NZ, NY, NX, NC = 16, 4, 4, 2
NQ = 4
F32, BF16 = jnp.float32, jnp.bfloat16
SHIFT = 4096.0
LOG_SHIFT = 8.317766166719343
WIDE_SHIFT = 16384.0
LOG_WIDE_SHIFT = 9.704060527839234


def encode(x):
    s = x * SHIFT
    s2 = s * s
    return (s2 * s2 * s).astype(BF16)


def decode(y):
    y = y.astype(F32)
    r = jnp.exp(jnp.log(jnp.abs(y)) * 0.2 - LOG_SHIFT)
    return jnp.where(y < 0, -r, r)


def encode_wide(x):
    s = x * WIDE_SHIFT
    return (s * s * s).astype(BF16)


def decode_wide(y):
    y = y.astype(F32)
    r = jnp.exp(jnp.log(jnp.abs(y)) * (1.0 / 3.0) - LOG_WIDE_SHIFT)
    return jnp.where(y < 0, -r, r)


def hops(d, n):
    return min(d, n - d)


def dot(a, b, dims, **kw):
    return lax.dot_general(a, b, (dims, ((), ())), preferred_element_type=F32, **kw)


def comm_kernel(
    scale, total, g_hbm, b_hbm, scores_ref, gram_ref,
    bbuf, gbuf, tf, ysend, yrecv, sf, zsend, zrecv, lall,
    spart, crecv, xsend, xrecv, sall, gp, gprecv, gzall,
    load_sem, out_sem, known, ys, yr, zs, zr, ls, lr, us, ur, cs, cr, xs, xr, ps, pr,
):
    samp, var = lax.axis_index("samples"), lax.axis_index("variants")
    z, y = lax.div(samp, NY), lax.rem(samp, NY)
    x, c = lax.div(var, NC), lax.rem(var, NC)
    odd = lax.rem(z, 2)

    def dev(dz, dy, dx, dc):
        return (
            lax.rem(z + dz, NZ) * NY + lax.rem(y + dy, NY),
            lax.rem(x + dx, NX) * NC + lax.rem(c + dc, NC),
        )

    def start(src, dst, send, recv, to):
        pltpu.make_async_remote_copy(
            src_ref=src, dst_ref=dst, send_sem=send, recv_sem=recv,
            device_id=to, device_id_type=MESH,
        ).start()

    def wait(ref, sem):
        pltpu.make_async_copy(ref, ref, sem).wait()

    def signal(sem, to):
        pl.semaphore_signal(sem, inc=1, device_id=to, device_id_type=MESH)

    def rows(i, n):
        return pl.ds(pl.multiple_of(i * n, n), n)

    plane = [(dy, dx, dc) for dy in range(NY) for dx in range(NX) for dc in range(NC)][1:]
    plane.sort(key=lambda p: -hops(p[0], NY) - hops(p[1], NX))
    far = sorted(range(1, NZ), key=lambda d: -hops(d, NZ))
    near = [(dz, 0, 0, 0) for dz in (2, 14, 1, 15)] + [(0, dy, 0, 0) for dy in (2, 1, 3)]
    near += [(0, 0, dx, 0) for dx in (2, 1, 3)] + [(0, 0, 0, 1)]
    units = [(q, h) for q in range(NQ) for h in range(2)]

    load_b = pltpu.make_async_copy(b_hbm, bbuf, load_sem.at[NQ])
    load_b.start()
    cols = gbuf.shape[2]
    loads = [
        pltpu.make_async_copy(g_hbm.at[:, pl.ds(q * cols, cols)], gbuf.at[q], load_sem.at[q])
        for q in range(NQ)
    ]
    for load in loads:
        load.start()
    barrier = pltpu.get_barrier_semaphore()
    for p in near:
        signal(barrier, dev(*p))

    def term(q):
        loads[q].wait()
        t = dot(bbuf[...], gbuf[q], ((0,), (0,)))
        for i in range(NY):
            tf[q, i] = t[:, i * 128:(i + 1) * 128]

    def send_y(q):
        for h in range(2):
            for dy in (2, 1, 3):
                to = lax.rem(y + dy, NY)
                ysend[q, h, dy - 1] = encode(tf[q, to, h * 128:(h + 1) * 128])
                start(ysend.at[q, h, dy - 1], yrecv.at[q, h, dy - 1], ys.at[q], yr.at[q, h], dev(0, dy, 0, 0))

    load_b.wait()
    term(0)
    pl.semaphore_wait(barrier, len(near))
    for dz in (2, 14):
        signal(known.at[0], dev(dz, 0, 0, 0))
    send_y(0)
    term(1)
    send_y(1)
    pl.semaphore_wait(known.at[0], 2)
    for dz in (4, 12):
        signal(known.at[1], dev(dz, 0, 0, 0))
    for q in range(2, NQ):
        term(q)
        send_y(q)
    pl.semaphore_wait(known.at[1], 2)
    for q, h in units:
        wait(yrecv.at[q, h], yr.at[q, h])
        s = tf[q, y, h * 128:(h + 1) * 128]
        for i in range(NY - 1):
            s = s + decode(yrecv[q, h, i])
        sf[q, h] = s
        zsend[q, h] = encode(s)
        par = lax.rem(z + h, 2)
        for i in (4, 3, 5, 2, 6, 1, 7, 0):
            def send_tile(i=i):
                d = 2 * i + par
                to = lax.rem(z + d, NZ)
                start(
                    zsend.at[q, h, rows(lax.div(to, 2), 16)], zrecv.at[q, rows(d - 1, 16)],
                    zs.at[q], zr.at[q], dev(d, 0, 0, 0),
                )
            if i:
                send_tile()
            else:
                pl.when(par == 1)(send_tile)
    tile = odd * 8 + lax.div(z, 2)
    for q in range(NQ):
        wait(zrecv.at[q], zr.at[q])
        s = sf[q, odd, rows(lax.div(z, 2), 16)]
        for i in range(NZ - 1):
            s = s + decode(zrecv[q, i * 16:(i + 1) * 16])
        lall[q, y, rows(tile, 16)] = s.astype(BF16)
        for dz in far:
            mine = lall.at[q, y, rows(tile, 16)]
            start(mine, mine, ls.at[q], lr.at[q, odd], dev(dz, 0, 0, 0))
    for q, h in units:
        @pl.when(odd == h)
        def _():
            wait(lall.at[q, y, pl.ds(0, 112)], lr.at[q, h])

        @pl.when(odd != h)
        def _():
            wait(lall.at[q, y, pl.ds(0, 128)], lr.at[q, h])

        for dy in (2, 1, 3):
            mine = lall.at[q, y, pl.ds(h * 128, 128)]
            start(mine, mine, us.at[q], ur.at[q, h], dev(0, dy, 0, 0))
    half, chunk = spart.shape[1] // NC, spart.shape[1] // (NC * NX)
    other = lax.rem(c + 1, NC)
    for q, h in units:
        wait(yrecv.at[q, h], ur.at[q, h])
        part = jnp.concatenate([lall[q, i, h * 128:(h + 1) * 128] for i in range(NY)], axis=1)
        t = dot(gbuf[q], part, ((1,), (1,)))
        if q == 0:
            spart[h] = t
        else:
            spart[h] += t
        if q == NQ - 1:
            start(spart.at[h, rows(other, half)], crecv.at[h], cs.at[h], cr.at[h], dev(0, 0, 0, 1))
    for h in range(2):
        wait(crecv.at[h], cr.at[h])
        crecv[h] = crecv[h] + spart[h, rows(c, half)]
        xsend[h] = encode_wide(crecv[h])
        for dx in (2, 1, 3):
            to = lax.rem(x + dx, NX)
            start(xsend.at[h, rows(to, chunk)], xrecv.at[h, dx - 1], xs.at[h], xr.at[h], dev(0, 0, dx, 0))
    mine = c * NX + x
    r = []
    for h in range(2):
        wait(xrecv.at[h], xr.at[h])
        s = crecv[h, rows(x, chunk)]
        for i in range(NX - 1):
            s = s + decode_wide(xrecv[h, i])
        r.append(s * scale)
    r = jnp.concatenate(r, axis=1)
    sall[rows(mine, chunk)] = r
    gp[...] = dot(r, r, ((0,), (0,)), precision=lax.Precision.HIGHEST) * (1.0 / total)

    def each_core(core, body):
        @pl.when(core == 0)
        def _():
            body(slice(None))

        @pl.when(core == 1)
        def _():
            body(pl.ds(128, 128))

    spot = (c * NX + x) * NY + y
    for i, (dy, dx, dc) in enumerate(plane):
        to = (lax.rem(c + dc, NC) * NX + lax.rem(x + dx, NX)) * NY + lax.rem(y + dy, NY)

        def send_part(lanes, i=i, to=to, p=(dy, dx, dc)):
            start(gp.at[rows(to, 8), lanes], gprecv.at[i, :, lanes], ps.at[2], pr.at[2], dev(0, *p))

        each_core(lax.rem(c + dc, NC), send_part)

    def sum_plane(lanes):
        wait(gprecv.at[:, :, lanes], pr.at[2])
        s = gp[rows(spot, 8), lanes]
        for i in range(len(plane)):
            s = s + gprecv[i, :, lanes]
        gzall[z, :, lanes] = s
        for dz in far:
            own = gzall.at[z, :, lanes]
            start(own, own, ps.at[6], pr.at[6], dev(dz, 0, 0, 0))

    each_core(c, sum_plane)
    for dx in (2, 1, 3):
        own = sall.at[rows(mine, chunk)]
        start(own, own, ps.at[4], pr.at[4], dev(0, 0, dx, 0))

    def sum_z(lanes):
        wait(gzall.at[pl.ds(0, NZ - 1), :, lanes], pr.at[6])
        s = gzall[0, :, lanes]
        for i in range(1, NZ):
            s = s + gzall[i, :, lanes]
        own = gram_ref.at[rows(spot, 8), lanes]
        own[...] = s
        for p in plane:
            start(own, own, ps.at[8], pr.at[8], dev(0, *p))

    each_core(c, sum_z)
    gram_ref[128:, :128] = jnp.zeros((128, 128), F32)
    wait(sall.at[pl.ds(0, 3 * chunk)], pr.at[4])
    own = sall.at[rows(c, half)]
    start(own, own, ps.at[7], pr.at[7], dev(0, 0, 0, 1))
    keep = pltpu.make_async_copy(own, scores_ref.at[rows(c, half)], out_sem.at[0])
    keep.start()
    wait(sall.at[pl.ds(0, half)], pr.at[7])
    own = sall.at[rows(other, half)]
    keep2 = pltpu.make_async_copy(own, scores_ref.at[rows(other, half)], out_sem.at[1])
    keep2.start()
    keep.wait()
    keep2.wait()

    @pl.when(c == 0)
    def _():
        wait(spart.at[0, pl.ds(0, 368)], pr.at[8])

    @pl.when(c == 1)
    def _():
        wait(spart.at[0, pl.ds(0, 376)], pr.at[8])

    for q in range(NQ):
        wait(ysend.at[q], ys.at[q])
        wait(zrecv.at[q], zs.at[q])
        wait(zrecv.at[q], ls.at[q])
        wait(lall.at[q, pl.ds(0, 3)], us.at[q])
    for h in range(2):
        wait(crecv.at[h], cs.at[h])
        wait(xrecv.at[h], xs.at[h])
    wait(sall.at[pl.ds(0, 3 * chunk)], ps.at[4])
    wait(sall.at[pl.ds(0, half)], ps.at[7])

    def sent(lanes):
        wait(gzall.at[pl.ds(0, NZ - 1), :, lanes], ps.at[6])
        wait(gprecv.at[:, :, lanes], ps.at[8])

    each_core(c, sent)

    @pl.when(c == 0)
    def _():
        wait(spart.at[0, pl.ds(0, 368)], ps.at[2])

    @pl.when(c == 1)
    def _():
        wait(spart.at[0, pl.ds(0, 376)], ps.at[2])


def scores_and_gram(genotypes, basis_in):
    n, v = genotypes.shape
    k = basis_in.shape[1]
    total_samples = n * lax.axis_size("samples")
    scale = 1.0 / (v * lax.axis_size("variants")) ** 0.5
    part = v // NQ
    chunk = n // (NC * NX)
    dma = pltpu.SemaphoreType.DMA
    vmem = pl.BlockSpec(memory_space=pltpu.VMEM)
    return pl.pallas_call(
        functools.partial(comm_kernel, scale, total_samples),
        out_shape=[jax.ShapeDtypeStruct((n, k), F32), jax.ShapeDtypeStruct((k, k), F32)],
        in_specs=[pl.BlockSpec(memory_space=pl.ANY)] * 2,
        out_specs=[pl.BlockSpec(memory_space=pl.ANY), vmem],
        scratch_shapes=[
            pltpu.VMEM((n, k), BF16),
            pltpu.VMEM((NQ, n, part), BF16),
            pltpu.VMEM((NQ, NY, k, 128), F32),
            pltpu.VMEM((NQ, 2, NY - 1, k // 2, 128), BF16),
            pltpu.VMEM((NQ, 2, NY - 1, k // 2, 128), BF16),
            pltpu.VMEM((NQ, 2, k // 2, 128), F32),
            pltpu.VMEM((NQ, 2, k // 2, 128), BF16),
            pltpu.VMEM((NQ, (NZ - 1) * 16, 128), BF16),
            pltpu.VMEM((NQ, NY, k, 128), BF16),
            pltpu.VMEM((2, n, k // 2), F32),
            pltpu.VMEM((2, n // NC, k // 2), F32),
            pltpu.VMEM((2, n // NC, k // 2), BF16),
            pltpu.VMEM((2, NX - 1, chunk, k // 2), BF16),
            pltpu.VMEM((n, k), F32),
            pltpu.VMEM((k, k), F32),
            pltpu.VMEM((NX * NY * NC - 1, 8, k), F32),
            pltpu.VMEM((NZ, 8, k), F32),
            dma((NQ + 1,)), dma((2,)), pltpu.SemaphoreType.REGULAR((2,)),
            dma((NQ,)), dma((NQ, 2)), dma((NQ,)), dma((NQ,)),
            dma((NQ,)), dma((NQ, 2)), dma((NQ,)), dma((NQ, 2)),
            dma((2,)), dma((2,)), dma((2,)), dma((2,)),
            dma((9,)), dma((9,)),
        ],
        compiler_params=pltpu.CompilerParams(
            collective_id=0, has_side_effects=True, vmem_limit_bytes=24 << 20
        ),
        cost_estimate=pl.CostEstimate(flops=4 * n * v * k, bytes_accessed=2 * n * v, transcendentals=0),
        name="scores_and_gram",
    )(*(pltpu.with_memory_space_constraint(a, pltpu.HBM) for a in (genotypes, basis_in)))


def eliminate(a, panel):
    n = a.shape[0]
    row, col = (lax.broadcasted_iota(jnp.int32, (n, n), i) for i in (0, 1))
    eye = jnp.where(row == col, 1.0, 0.0)
    sub = lax.broadcasted_iota(jnp.int32, (8, n), 0)
    left = [a[8 * i:8 * i + 8] for i in range(n // 8)]
    right = [eye[8 * i:8 * i + 8] for i in range(n // 8)]
    upper, inverse = [], []
    for j0 in range(0, n, panel):
        lo = j0 // 8
        cols = [
            [jnp.broadcast_to(g[:, j0 + k:j0 + k + 1], (8, n)) for g in left[lo:]]
            for k in range(panel)
        ]
        for k in range(panel):
            j = j0 + k
            v, s = j // 8, j % 8
            pivot = cols[k][v - lo][s:s + 1]
            inv = 1.0 / pivot
            root = lax.rsqrt(pivot)
            ra, rb = left[v][s:s + 1], right[v][s:s + 1]
            upper.append(ra * root)
            inverse.append(rb * root)
            if j == n - 1:
                break
            sa = jnp.broadcast_to(ra * inv, (8, n))
            sb = jnp.broadcast_to(rb * inv, (8, n))
            sc = [jnp.broadcast_to(cols[m][v - lo][s:s + 1] * inv, (8, n)) for m in range(k + 1, panel)]
            for i in range(v if s < 7 else v + 1, n // 8):
                c = cols[k][i - lo]
                if i == v:
                    c = jnp.where(sub > s, c, 0.0)
                left[i] = left[i] - c * sa
                right[i] = right[i] - c * sb
                for m in range(k + 1, panel):
                    cols[m][i - lo] = cols[m][i - lo] - c * sc[m - k - 1]
    upper = jnp.where(row <= col, jnp.concatenate(upper, axis=0), 0.0)
    inverse = jnp.where(row >= col, jnp.concatenate(inverse, axis=0), 0.0)
    return upper, inverse


def split(a):
    high = a.astype(BF16)
    return high, (a - high.astype(F32)).astype(BF16)


def dot3(a, b, dims):
    (ah, al), (bh, bl) = split(a), split(b)
    return dot(ah, bh, dims) + (dot(ah, bl, dims) + dot(al, bh, dims))


def factor_kernel(panel, gram, scores_hbm, basis_hbm, factor, scores, basis, sems):
    n = gram.shape[0]
    h = n // 2
    load = pltpu.make_async_copy(scores_hbm, scores, sems.at[0])
    load.start()
    u11, v1 = eliminate(gram[:h, :h], panel)
    load.wait()
    u12 = dot(v1, gram[:h, h:], ((1,), (0,)), precision=lax.Precision.HIGHEST)
    a22 = gram[h:, h:] - dot(u12, u12, ((0,), (0,)), precision=lax.Precision.HIGHEST)
    first = dot3(scores[:, :h], v1, ((1,), (1,)))
    rest = scores[:, h:] - dot3(first, u12, ((1,), (0,)))
    u22, v2 = eliminate(a22, panel)
    basis[0] = first
    basis[1] = dot3(rest, v2, ((1,), (1,)))
    out1 = pltpu.make_async_copy(basis.at[0], basis_hbm.at[:, pl.ds(0, h)], sems.at[1])
    out1.start()
    out2 = pltpu.make_async_copy(basis.at[1], basis_hbm.at[:, pl.ds(h, h)], sems.at[2])
    out2.start()
    factor[:h, :h] = u11
    factor[:h, h:] = u12
    factor[h:, :h] = jnp.zeros((h, h), F32)
    factor[h:, h:] = u22
    out1.wait()
    out2.wait()


def factor_and_basis(gram, scores):
    n, k = scores.shape
    vmem, hbm = pl.BlockSpec(memory_space=pltpu.VMEM), pl.BlockSpec(memory_space=pltpu.HBM)
    return pl.pallas_call(
        functools.partial(factor_kernel, 8),
        out_shape=[jax.ShapeDtypeStruct(scores.shape, F32), jax.ShapeDtypeStruct(gram.shape, F32)],
        in_specs=[vmem, hbm],
        out_specs=[hbm, vmem],
        scratch_shapes=[
            pltpu.VMEM((n, k), F32),
            pltpu.VMEM((2, n, k // 2), F32),
            pltpu.SemaphoreType.DMA((3,)),
        ],
        compiler_params=pltpu.CompilerParams(vmem_limit_bytes=40 << 20),
        name="factor_and_basis",
    )(gram, scores)


def local(genotypes, basis_in):
    scores, gram = scores_and_gram(genotypes, basis_in)
    return tuple(factor_and_basis(gram, scores))


def solution(mesh):
    placed = (P("samples", "variants"), P("samples", None))
    return jax.shard_map(
        local, mesh=mesh, in_specs=placed, out_specs=(P("samples", None), P()), check_vma=False
    )
```

```python
import functools

import jax
import jax.numpy as jnp
from jax import lax
from jax.experimental import pallas as pl
from jax.experimental.pallas import tpu as pltpu
from jax.sharding import PartitionSpec as P

MESH = pl.DeviceIdType.MESH
NZ, NY, NX, NC = 16, 4, 4, 2
NQ = 4
F32, BF16 = jnp.float32, jnp.bfloat16
SHIFT = 4096.0
LOG_SHIFT = 8.317766166719343
WIDE_SHIFT = 16384.0
LOG_WIDE_SHIFT = 9.704060527839234


def encode(x):
    s = x * SHIFT
    s2 = s * s
    return (s2 * s2 * s).astype(BF16)


def decode(y):
    y = y.astype(F32)
    r = jnp.exp(jnp.log(jnp.abs(y)) * 0.2 - LOG_SHIFT)
    return jnp.where(y < 0, -r, r)


def encode_wide(x):
    s = x * WIDE_SHIFT
    return (s * s * s).astype(BF16)


def decode_wide(y):
    y = y.astype(F32)
    r = jnp.exp(jnp.log(jnp.abs(y)) * (1.0 / 3.0) - LOG_WIDE_SHIFT)
    return jnp.where(y < 0, -r, r)


def hops(d, n):
    return min(d, n - d)


def dot(a, b, dims, **kw):
    return lax.dot_general(a, b, (dims, ((), ())), preferred_element_type=F32, **kw)


def comm_kernel(
    scale, total, g_hbm, b_hbm, scores_ref, gram_ref,
    bbuf, gbuf, tf, psend, precv, ysend, yrecv, sf, zsend, zrecv, lall,
    spart, crecv, xsend, xrecv, sall, gp, gprecv, gzall,
    load_sem, out_sem, known, ks, kr, ys, yr, zs, zr, ls, lr, us, ur, ws, wr, cs, cr, xs, xr, ps, pr,
):
    samp, var = lax.axis_index("samples"), lax.axis_index("variants")
    z, y = lax.div(samp, NY), lax.rem(samp, NY)
    x, c = lax.div(var, NC), lax.rem(var, NC)
    pair = lax.div(z, 2)

    def dev(dz, dy, dx, dc):
        return (
            lax.rem(z + dz, NZ) * NY + lax.rem(y + dy, NY),
            lax.rem(x + dx, NX) * NC + lax.rem(c + dc, NC),
        )

    def start(src, dst, send, recv, to):
        pltpu.make_async_remote_copy(
            src_ref=src, dst_ref=dst, send_sem=send, recv_sem=recv,
            device_id=to, device_id_type=MESH,
        ).start()

    def wait(ref, sem):
        pltpu.make_async_copy(ref, ref, sem).wait()

    def signal(sem, to):
        pl.semaphore_signal(sem, inc=1, device_id=to, device_id_type=MESH)

    def rows(i, n):
        return pl.ds(pl.multiple_of(i * n, n), n)

    plane = [(dy, dx, dc) for dy in range(NY) for dx in range(NX) for dc in range(NC)][1:]
    plane.sort(key=lambda p: -hops(p[0], NY) - hops(p[1], NX))
    far = sorted(range(1, NZ), key=lambda d: -hops(d, NZ))
    near = [(dz, 0, 0, 0) for dz in (2, 14, 1, 15)] + [(0, dy, 0, 0) for dy in (2, 1, 3)]
    near += [(0, 0, dx, 0) for dx in (2, 1, 3)] + [(0, 0, 0, 1)]

    load_b = pltpu.make_async_copy(b_hbm, bbuf, load_sem.at[NQ])
    load_b.start()
    cols = gbuf.shape[2]
    loads = [
        pltpu.make_async_copy(g_hbm.at[:, pl.ds(q * cols, cols)], gbuf.at[q], load_sem.at[q])
        for q in range(NQ)
    ]
    for load in loads:
        load.start()
    barrier = pltpu.get_barrier_semaphore()
    for p in near:
        signal(barrier, dev(*p))

    def term(q):
        loads[q].wait()
        t = dot(bbuf[...], gbuf[q], ((0,), (0,)))
        for i in range(NY):
            tf[q, i] = t[:, i * 128:(i + 1) * 128]

    units = [(q, h) for q in range(NQ) for h in range(2)]

    def parity(h):
        return lax.rem(z + h, 2)

    def partner(h):
        return dev(1 + 14 * parity(h), 0, 0, 0)

    def keep(h):
        return rows(2 * h + parity(h), 64)

    def send_pair(q):
        for h in range(2):
            for i in range(NY):
                psend[q, h, i] = encode(tf[q, i, rows(2 * h + 1 - parity(h), 64)])
            start(psend.at[q, h], precv.at[q, h], ks.at[q], kr.at[q, h], partner(h))

    def send_y(q, h):
        wait(precv.at[q, h], kr.at[q, h])
        for dy in (2, 1, 3, 0):
            to = lax.rem(y + dy, NY)
            s = tf[q, to, keep(h)] + decode(precv[q, h, to])
            if dy == 0:
                sf[q, h] = s
                continue
            ysend[q, h, dy - 1] = encode(s)
            start(ysend.at[q, h, dy - 1], yrecv.at[q, h, dy - 1], ys.at[q], yr.at[q, h], dev(0, dy, 0, 0))

    def send_z(q, h):
        wait(yrecv.at[q, h], yr.at[q, h])
        s = sf[q, h]
        for i in range(NY - 1):
            s = s + decode(yrecv[q, h, i])
        sf[q, h] = s
        zsend[q, h] = encode(s)
        shift = lax.rem(pair + q, 2)
        for i in (2, 1, 3, 0):
            def send_tile(i=i):
                d = 2 * i + shift
                to = lax.div(lax.rem(pair + d, 8), 2)
                start(
                    zsend.at[q, h, rows(to, 16)], zrecv.at[q, h, rows(d - 1, 16)],
                    zs.at[q], zr.at[q, h], dev(2 * d, 0, 0, 0),
                )
            if i:
                send_tile()
            else:
                pl.when(shift == 1)(send_tile)

    def finish_tile(q, h):
        @pl.when(lax.rem(pair + q, 2) == 0)
        def _():
            wait(zrecv.at[q, h], zr.at[q, h])
            s = sf[q, h, rows(lax.div(pair, 2), 16)]
            for i in range(7):
                s = s + decode(zrecv[q, h, i * 16:(i + 1) * 16])
            tile = rows(8 * h + 4 * parity(h) + lax.div(pair, 2), 16)
            lall[q, y, tile] = s.astype(BF16)
            for d in (4, 3, 5, 2, 6, 1, 7):
                mine = lall.at[q, y, tile]
                start(mine, mine, ls.at[q], lr.at[q, h], dev(2 * d, 0, 0, 0))

    def gather_y(q, h):
        @pl.when(lax.rem(pair + q, 2) == 0)
        def _():
            wait(lall.at[q, y, pl.ds(0, 48)], lr.at[q, h])

        @pl.when(lax.rem(pair + q, 2) == 1)
        def _():
            wait(lall.at[q, y, pl.ds(0, 64)], lr.at[q, h])

        for dy in (2, 1, 3):
            mine = lall.at[q, y, keep(h)]
            start(mine, mine, us.at[q], ur.at[q, h], dev(0, dy, 0, 0))

    def gather_pair(q, h):
        wait(yrecv.at[q, h], ur.at[q, h])
        mine = lall.at[q, :, keep(h)]
        start(mine, mine, ws.at[q], wr.at[q, h], partner(h))

    load_b.wait()
    term(0)
    pl.semaphore_wait(barrier, len(near))
    for dz in (2, 14):
        signal(known.at[0], dev(dz, 0, 0, 0))
    send_pair(0)
    term(1)
    send_pair(1)
    pl.semaphore_wait(known.at[0], 2)
    for dz in (4, 12):
        signal(known.at[1], dev(dz, 0, 0, 0))
    for q in range(2, NQ):
        term(q)
        send_pair(q)
    late = 5
    for u in range(len(units) + late):
        if u < len(units):
            send_y(*units[u])
        if u == late:
            pl.semaphore_wait(known.at[1], 2)
        if u >= late:
            send_z(*units[u - late])
    for u in units:
        finish_tile(*u)
    half, chunk = spart.shape[1] // NC, spart.shape[1] // (NC * NX)
    other = lax.rem(c + 1, NC)

    def score_term(q, h):
        wait(precv.at[q, h], wr.at[q, h])
        part = jnp.concatenate([lall[q, i, h * 128:(h + 1) * 128] for i in range(NY)], axis=1)
        t = dot(gbuf[q], part, ((1,), (1,)))
        if q == 0:
            spart[h] = t
        else:
            spart[h] += t
        if q == NQ - 1:
            start(spart.at[h, rows(other, half)], crecv.at[h], cs.at[h], cr.at[h], dev(0, 0, 0, 1))

    for u in range(len(units) + 9):
        if u < len(units):
            gather_y(*units[u])
        if 5 <= u < len(units) + 5:
            gather_pair(*units[u - 5])
        if u >= 9:
            score_term(*units[u - 9])
    for h in range(2):
        wait(crecv.at[h], cr.at[h])
        crecv[h] = crecv[h] + spart[h, rows(c, half)]
        xsend[h] = encode_wide(crecv[h])
        for dx in (2, 1, 3):
            to = lax.rem(x + dx, NX)
            start(xsend.at[h, rows(to, chunk)], xrecv.at[h, dx - 1], xs.at[h], xr.at[h], dev(0, 0, dx, 0))
    mine = c * NX + x
    r = []
    for h in range(2):
        wait(xrecv.at[h], xr.at[h])
        s = crecv[h, rows(x, chunk)]
        for i in range(NX - 1):
            s = s + decode_wide(xrecv[h, i])
        r.append(s * scale)
    r = jnp.concatenate(r, axis=1)
    sall[rows(mine, chunk)] = r
    gp[...] = dot(r, r, ((0,), (0,)), precision=lax.Precision.HIGHEST) * (1.0 / total)

    def each_core(core, body):
        @pl.when(core == 0)
        def _():
            body(slice(None))

        @pl.when(core == 1)
        def _():
            body(pl.ds(128, 128))

    spot = (c * NX + x) * NY + y
    for i, (dy, dx, dc) in enumerate(plane):
        to = (lax.rem(c + dc, NC) * NX + lax.rem(x + dx, NX)) * NY + lax.rem(y + dy, NY)

        def send_part(lanes, i=i, to=to, p=(dy, dx, dc)):
            start(gp.at[rows(to, 8), lanes], gprecv.at[i, :, lanes], ps.at[2], pr.at[2], dev(0, *p))

        each_core(lax.rem(c + dc, NC), send_part)

    def sum_plane(lanes):
        wait(gprecv.at[:, :, lanes], pr.at[2])
        s = gp[rows(spot, 8), lanes]
        for i in range(len(plane)):
            s = s + gprecv[i, :, lanes]
        gzall[z, :, lanes] = s
        for dz in far:
            own = gzall.at[z, :, lanes]
            start(own, own, ps.at[6], pr.at[6], dev(dz, 0, 0, 0))

    each_core(c, sum_plane)
    for dx in (2, 1, 3):
        own = sall.at[rows(mine, chunk)]
        start(own, own, ps.at[4], pr.at[4], dev(0, 0, dx, 0))

    def sum_z(lanes):
        wait(gzall.at[pl.ds(0, NZ - 1), :, lanes], pr.at[6])
        s = gzall[0, :, lanes]
        for i in range(1, NZ):
            s = s + gzall[i, :, lanes]
        own = gram_ref.at[rows(spot, 8), lanes]
        own[...] = s
        for p in plane:
            start(own, own, ps.at[8], pr.at[8], dev(0, *p))

    each_core(c, sum_z)
    gram_ref[128:, :128] = jnp.zeros((128, 128), F32)
    wait(sall.at[pl.ds(0, 3 * chunk)], pr.at[4])
    own = sall.at[rows(c, half)]
    start(own, own, ps.at[7], pr.at[7], dev(0, 0, 0, 1))
    out1 = pltpu.make_async_copy(own, scores_ref.at[rows(c, half)], out_sem.at[0])
    out1.start()
    wait(sall.at[pl.ds(0, half)], pr.at[7])
    own = sall.at[rows(other, half)]
    out2 = pltpu.make_async_copy(own, scores_ref.at[rows(other, half)], out_sem.at[1])
    out2.start()
    out1.wait()
    out2.wait()

    @pl.when(c == 0)
    def _():
        wait(spart.at[0, pl.ds(0, 368)], pr.at[8])

    @pl.when(c == 1)
    def _():
        wait(spart.at[0, pl.ds(0, 376)], pr.at[8])

    for q in range(NQ):
        wait(psend.at[q], ks.at[q])
        wait(ysend.at[q], ys.at[q])
        wait(ysend.at[q], us.at[q])
        wait(psend.at[q], ws.at[q])

        @pl.when(lax.rem(pair + q, 2) == 0)
        def _():
            wait(lall.at[q, 0, pl.ds(0, 96)], zs.at[q])
            wait(zrecv.at[q], ls.at[q])

        @pl.when(lax.rem(pair + q, 2) == 1)
        def _():
            wait(lall.at[q, 0, pl.ds(0, 128)], zs.at[q])

    for h in range(2):
        wait(crecv.at[h], cs.at[h])
        wait(xrecv.at[h], xs.at[h])
    wait(sall.at[pl.ds(0, 3 * chunk)], ps.at[4])
    wait(sall.at[pl.ds(0, half)], ps.at[7])

    def sent(lanes):
        wait(gzall.at[pl.ds(0, NZ - 1), :, lanes], ps.at[6])
        wait(gprecv.at[:, :, lanes], ps.at[8])

    each_core(c, sent)

    @pl.when(c == 0)
    def _():
        wait(spart.at[0, pl.ds(0, 368)], ps.at[2])

    @pl.when(c == 1)
    def _():
        wait(spart.at[0, pl.ds(0, 376)], ps.at[2])


def scores_and_gram(genotypes, basis_in):
    n, v = genotypes.shape
    k = basis_in.shape[1]
    total_samples = n * lax.axis_size("samples")
    scale = 1.0 / (v * lax.axis_size("variants")) ** 0.5
    part = v // NQ
    chunk = n // (NC * NX)
    dma = pltpu.SemaphoreType.DMA
    vmem = pl.BlockSpec(memory_space=pltpu.VMEM)
    return pl.pallas_call(
        functools.partial(comm_kernel, scale, total_samples),
        out_shape=[jax.ShapeDtypeStruct((n, k), F32), jax.ShapeDtypeStruct((k, k), F32)],
        in_specs=[pl.BlockSpec(memory_space=pl.ANY)] * 2,
        out_specs=[pl.BlockSpec(memory_space=pl.ANY), vmem],
        scratch_shapes=[
            pltpu.VMEM((n, k), BF16),
            pltpu.VMEM((NQ, n, part), BF16),
            pltpu.VMEM((NQ, NY, k, 128), F32),
            pltpu.VMEM((NQ, 2, NY, k // 4, 128), BF16),
            pltpu.VMEM((NQ, 2, NY, k // 4, 128), BF16),
            pltpu.VMEM((NQ, 2, NY - 1, k // 4, 128), BF16),
            pltpu.VMEM((NQ, 2, NY - 1, k // 4, 128), BF16),
            pltpu.VMEM((NQ, 2, k // 4, 128), F32),
            pltpu.VMEM((NQ, 2, k // 4, 128), BF16),
            pltpu.VMEM((NQ, 2, 7 * 16, 128), BF16),
            pltpu.VMEM((NQ, NY, k, 128), BF16),
            pltpu.VMEM((2, n, k // 2), F32),
            pltpu.VMEM((2, n // NC, k // 2), F32),
            pltpu.VMEM((2, n // NC, k // 2), BF16),
            pltpu.VMEM((2, NX - 1, chunk, k // 2), BF16),
            pltpu.VMEM((n, k), F32),
            pltpu.VMEM((k, k), F32),
            pltpu.VMEM((NX * NY * NC - 1, 8, k), F32),
            pltpu.VMEM((NZ, 8, k), F32),
            dma((NQ + 1,)), dma((2,)), pltpu.SemaphoreType.REGULAR((2,)),
            dma((NQ,)), dma((NQ, 2)), dma((NQ,)), dma((NQ, 2)), dma((NQ,)), dma((NQ, 2)),
            dma((NQ,)), dma((NQ, 2)), dma((NQ,)), dma((NQ, 2)), dma((NQ,)), dma((NQ, 2)),
            dma((2,)), dma((2,)), dma((2,)), dma((2,)),
            dma((9,)), dma((9,)),
        ],
        compiler_params=pltpu.CompilerParams(
            collective_id=0, has_side_effects=True, vmem_limit_bytes=24 << 20
        ),
        cost_estimate=pl.CostEstimate(flops=4 * n * v * k, bytes_accessed=2 * n * v, transcendentals=0),
        name="scores_and_gram",
    )(*(pltpu.with_memory_space_constraint(a, pltpu.HBM) for a in (genotypes, basis_in)))


def eliminate(a, panel):
    n = a.shape[0]
    row, col = (lax.broadcasted_iota(jnp.int32, (n, n), i) for i in (0, 1))
    eye = jnp.where(row == col, 1.0, 0.0)
    sub = lax.broadcasted_iota(jnp.int32, (8, n), 0)
    left = [a[8 * i:8 * i + 8] for i in range(n // 8)]
    right = [eye[8 * i:8 * i + 8] for i in range(n // 8)]
    upper, inverse = [], []
    for j0 in range(0, n, panel):
        lo = j0 // 8
        cols = [
            [jnp.broadcast_to(g[:, j0 + k:j0 + k + 1], (8, n)) for g in left[lo:]]
            for k in range(panel)
        ]
        for k in range(panel):
            j = j0 + k
            v, s = j // 8, j % 8
            pivot = cols[k][v - lo][s:s + 1]
            inv = 1.0 / pivot
            root = lax.rsqrt(pivot)
            ra, rb = left[v][s:s + 1], right[v][s:s + 1]
            upper.append(ra * root)
            inverse.append(rb * root)
            if j == n - 1:
                break
            sa = jnp.broadcast_to(ra * inv, (8, n))
            sb = jnp.broadcast_to(rb * inv, (8, n))
            sc = [jnp.broadcast_to(cols[m][v - lo][s:s + 1] * inv, (8, n)) for m in range(k + 1, panel)]
            for i in range(v if s < 7 else v + 1, n // 8):
                c = cols[k][i - lo]
                if i == v:
                    c = jnp.where(sub > s, c, 0.0)
                left[i] = left[i] - c * sa
                right[i] = right[i] - c * sb
                for m in range(k + 1, panel):
                    cols[m][i - lo] = cols[m][i - lo] - c * sc[m - k - 1]
    upper = jnp.where(row <= col, jnp.concatenate(upper, axis=0), 0.0)
    inverse = jnp.where(row >= col, jnp.concatenate(inverse, axis=0), 0.0)
    return upper, inverse


def split(a):
    high = a.astype(BF16)
    return high, (a - high.astype(F32)).astype(BF16)


def dot3(a, b, dims):
    (ah, al), (bh, bl) = split(a), split(b)
    return dot(ah, bh, dims) + (dot(ah, bl, dims) + dot(al, bh, dims))


def factor_kernel(panel, gram, scores_hbm, basis_hbm, factor, scores, basis, sems):
    n = gram.shape[0]
    h = n // 2
    load = pltpu.make_async_copy(scores_hbm, scores, sems.at[0])
    load.start()
    u11, v1 = eliminate(gram[:h, :h], panel)
    load.wait()
    u12 = dot(v1, gram[:h, h:], ((1,), (0,)), precision=lax.Precision.HIGHEST)
    a22 = gram[h:, h:] - dot(u12, u12, ((0,), (0,)), precision=lax.Precision.HIGHEST)
    first = dot3(scores[:, :h], v1, ((1,), (1,)))
    rest = scores[:, h:] - dot3(first, u12, ((1,), (0,)))
    u22, v2 = eliminate(a22, panel)
    basis[0] = first
    basis[1] = dot3(rest, v2, ((1,), (1,)))
    out1 = pltpu.make_async_copy(basis.at[0], basis_hbm.at[:, pl.ds(0, h)], sems.at[1])
    out1.start()
    out2 = pltpu.make_async_copy(basis.at[1], basis_hbm.at[:, pl.ds(h, h)], sems.at[2])
    out2.start()
    factor[:h, :h] = u11
    factor[:h, h:] = u12
    factor[h:, :h] = jnp.zeros((h, h), F32)
    factor[h:, h:] = u22
    out1.wait()
    out2.wait()


def factor_and_basis(gram, scores):
    n, k = scores.shape
    vmem, hbm = pl.BlockSpec(memory_space=pltpu.VMEM), pl.BlockSpec(memory_space=pltpu.HBM)
    return pl.pallas_call(
        functools.partial(factor_kernel, 8),
        out_shape=[jax.ShapeDtypeStruct(scores.shape, F32), jax.ShapeDtypeStruct(gram.shape, F32)],
        in_specs=[vmem, hbm],
        out_specs=[hbm, vmem],
        scratch_shapes=[
            pltpu.VMEM((n, k), F32),
            pltpu.VMEM((2, n, k // 2), F32),
            pltpu.SemaphoreType.DMA((3,)),
        ],
        compiler_params=pltpu.CompilerParams(vmem_limit_bytes=40 << 20),
        name="factor_and_basis",
    )(gram, scores)


def local(genotypes, basis_in):
    scores, gram = scores_and_gram(genotypes, basis_in)
    return tuple(factor_and_basis(gram, scores))


def solution(mesh):
    placed = (P("samples", "variants"), P("samples", None))
    return jax.shard_map(
        local, mesh=mesh, in_specs=placed, out_specs=(P("samples", None), P()), check_vma=False
    )
```

```python
import functools

import jax
import jax.numpy as jnp
from jax import lax
from jax.experimental import pallas as pl
from jax.experimental.pallas import tpu as pltpu
from jax.sharding import PartitionSpec as P

MESH = pl.DeviceIdType.MESH
NZ, NY, NX, NC = 16, 4, 4, 2
NQ = 4
F32, BF16 = jnp.float32, jnp.bfloat16
SHIFT = 4096.0
LOG_SHIFT = 8.317766166719343
WIDE_SHIFT = 16384.0
LOG_WIDE_SHIFT = 9.704060527839234


def encode(x):
    s = x * SHIFT
    s2 = s * s
    return (s2 * s2 * s).astype(BF16)


def decode(y):
    y = y.astype(F32)
    r = jnp.exp(jnp.log(jnp.abs(y)) * 0.2 - LOG_SHIFT)
    return jnp.where(y < 0, -r, r)


def encode_wide(x):
    s = x * WIDE_SHIFT
    return (s * s * s).astype(BF16)


def decode_wide(y):
    y = y.astype(F32)
    r = jnp.exp(jnp.log(jnp.abs(y)) * (1.0 / 3.0) - LOG_WIDE_SHIFT)
    return jnp.where(y < 0, -r, r)


def hops(d, n):
    return min(d, n - d)


def dot(a, b, dims, **kw):
    return lax.dot_general(a, b, (dims, ((), ())), preferred_element_type=F32, **kw)


def comm_kernel(
    scale, total, g_hbm, b_hbm, scores_ref, gram_ref,
    bbuf, gbuf, tf, psend, precv, ysend, yrecv, sf, zsend, zrecv, lall,
    spart, crecv, xsend, xrecv, sall, gp, gprecv, gzall,
    load_sem, out_sem, known, ks, kr, ys, yr, zs, zr, ls, lr, us, ur, ws, wr, cs, cr, xs, xr, ps, pr,
):
    samp, var = lax.axis_index("samples"), lax.axis_index("variants")
    z, y = lax.div(samp, NY), lax.rem(samp, NY)
    x, c = lax.div(var, NC), lax.rem(var, NC)
    pair = lax.div(z, 2)

    def dev(dz, dy, dx, dc):
        return (
            lax.rem(z + dz, NZ) * NY + lax.rem(y + dy, NY),
            lax.rem(x + dx, NX) * NC + lax.rem(c + dc, NC),
        )

    def start(src, dst, send, recv, to):
        pltpu.make_async_remote_copy(
            src_ref=src, dst_ref=dst, send_sem=send, recv_sem=recv,
            device_id=to, device_id_type=MESH,
        ).start()

    def wait(ref, sem):
        pltpu.make_async_copy(ref, ref, sem).wait()

    def signal(sem, to):
        pl.semaphore_signal(sem, inc=1, device_id=to, device_id_type=MESH)

    def rows(i, n):
        return pl.ds(pl.multiple_of(i * n, n), n)

    plane = [(dy, dx, dc) for dy in range(NY) for dx in range(NX) for dc in range(NC)][1:]
    plane.sort(key=lambda p: -hops(p[0], NY) - hops(p[1], NX))
    far = sorted(range(1, NZ), key=lambda d: -hops(d, NZ))
    near = [(dz, 0, 0, 0) for dz in (2, 14, 1, 15)] + [(0, dy, 0, 0) for dy in (2, 1, 3)]
    near += [(0, 0, dx, 0) for dx in (2, 1, 3)] + [(0, 0, 0, 1)]

    load_b = pltpu.make_async_copy(b_hbm, bbuf, load_sem.at[NQ])
    load_b.start()
    cols = gbuf.shape[2]
    loads = [
        pltpu.make_async_copy(g_hbm.at[:, pl.ds(q * cols, cols)], gbuf.at[q], load_sem.at[q])
        for q in range(NQ)
    ]
    for load in loads:
        load.start()
    barrier = pltpu.get_barrier_semaphore()
    for p in near:
        signal(barrier, dev(*p))

    def term(q):
        loads[q].wait()
        t = dot(bbuf[...], gbuf[q], ((0,), (0,)))
        for i in range(NY):
            tf[q, i] = t[:, i * 128:(i + 1) * 128]

    units = [(q, h) for q in range(NQ) for h in range(2)]

    def parity(h):
        return lax.rem(z + h, 2)

    def partner(h, dy=0):
        return dev(1 + 14 * parity(h), dy, 0, 0)

    def keep(h):
        return rows(2 * h + parity(h), 64)

    def send_pair(q):
        for h in range(2):
            for i in range(NY):
                psend[q, h, i] = encode(tf[q, i, rows(2 * h + 1 - parity(h), 64)])
            start(psend.at[q, h], precv.at[q, h], ks.at[q], kr.at[q, h], partner(h))

    def send_direct(q):
        for h in range(2):
            for dy in (2, 1, 3, 0):
                to = lax.rem(y + dy, NY)
                psend[q, h, dy] = encode(tf[q, to, rows(2 * h + 1 - parity(h), 64)])
                start(psend.at[q, h, dy], precv.at[q, h, dy], ks.at[q], kr.at[q, h], partner(h, dy))
            for dy in (2, 1, 3):
                to = lax.rem(y + dy, NY)
                ysend[q, h, dy - 1] = encode(tf[q, to, keep(h)])
                start(ysend.at[q, h, dy - 1], yrecv.at[q, h, dy - 1], ys.at[q], yr.at[q, h], dev(0, dy, 0, 0))

    def send_y(q, h):
        wait(precv.at[q, h], kr.at[q, h])
        for dy in (2, 1, 3, 0):
            to = lax.rem(y + dy, NY)
            s = tf[q, to, keep(h)] + decode(precv[q, h, to])
            if dy == 0:
                sf[q, h] = s
                continue
            ysend[q, h, dy - 1] = encode(s)
            start(ysend.at[q, h, dy - 1], yrecv.at[q, h, dy - 1], ys.at[q], yr.at[q, h], dev(0, dy, 0, 0))

    def send_z(q, h):
        wait(yrecv.at[q, h], yr.at[q, h])
        if q == NQ - 1:
            wait(precv.at[q, h], kr.at[q, h])
            s = tf[q, y, keep(h)]
            for i in range(NY):
                s = s + decode(precv[q, h, i])
        else:
            s = sf[q, h]
        for i in range(NY - 1):
            s = s + decode(yrecv[q, h, i])
        sf[q, h] = s
        zsend[q, h] = encode(s)
        shift = lax.rem(pair + q, 2)
        for i in (2, 1, 3, 0):
            def send_tile(i=i):
                d = 2 * i + shift
                to = lax.div(lax.rem(pair + d, 8), 2)
                start(
                    zsend.at[q, h, rows(to, 16)], zrecv.at[q, h, rows(d - 1, 16)],
                    zs.at[q], zr.at[q, h], dev(2 * d, 0, 0, 0),
                )
            if i:
                send_tile()
            else:
                pl.when(shift == 1)(send_tile)

    def finish_tile(q, h):
        @pl.when(lax.rem(pair + q, 2) == 0)
        def _():
            wait(zrecv.at[q, h], zr.at[q, h])
            s = sf[q, h, rows(lax.div(pair, 2), 16)]
            for i in range(7):
                s = s + decode(zrecv[q, h, i * 16:(i + 1) * 16])
            tile = rows(8 * h + 4 * parity(h) + lax.div(pair, 2), 16)
            lall[q, y, tile] = s.astype(BF16)
            for d in (4, 3, 5, 2, 6, 1, 7):
                mine = lall.at[q, y, tile]
                start(mine, mine, ls.at[q], lr.at[q, h], dev(2 * d, 0, 0, 0))

    def gather_y(q, h):
        @pl.when(lax.rem(pair + q, 2) == 0)
        def _():
            wait(lall.at[q, y, pl.ds(0, 48)], lr.at[q, h])

        @pl.when(lax.rem(pair + q, 2) == 1)
        def _():
            wait(lall.at[q, y, pl.ds(0, 64)], lr.at[q, h])

        mine = lall.at[q, y, keep(h)]
        if q == NQ - 1:
            for dy in (2, 1, 3, 0):
                start(mine, mine, ws.at[q], wr.at[q, h], partner(h, dy))
        for dy in (2, 1, 3):
            start(mine, mine, us.at[q], ur.at[q, h], dev(0, dy, 0, 0))

    def gather_pair(q, h):
        wait(yrecv.at[q, h], ur.at[q, h])
        mine = lall.at[q, :, keep(h)]
        start(mine, mine, ws.at[q], wr.at[q, h], partner(h))

    load_b.wait()
    term(0)
    pl.semaphore_wait(barrier, len(near))
    for dz in (2, 14):
        signal(known.at[0], dev(dz, 0, 0, 0))
    for dz in (1, 15):
        signal(known.at[2], dev(dz, 0, 0, 0))
    send_pair(0)
    term(1)
    send_pair(1)
    pl.semaphore_wait(known.at[0], 2)
    for dz in (4, 12):
        signal(known.at[1], dev(dz, 0, 0, 0))
    term(2)
    send_pair(2)
    term(3)
    pl.semaphore_wait(known.at[2], 2)
    send_direct(3)
    for u in range(5):
        send_y(*units[u])
    pl.semaphore_wait(known.at[1], 2)
    send_z(*units[0])
    send_y(*units[5])
    for u in range(1, 8):
        send_z(*units[u])
    for u in units:
        finish_tile(*u)
    half, chunk = spart.shape[1] // NC, spart.shape[1] // (NC * NX)
    other = lax.rem(c + 1, NC)

    def score_term(q, halves):
        for h in halves:
            if q == NQ - 1:
                wait(yrecv.at[q, h], ur.at[q, h])
            wait(precv.at[q, h], wr.at[q, h])
        lo, hi = 128 * halves[0], 128 * (halves[-1] + 1)
        part = jnp.concatenate([lall[q, i, lo:hi] for i in range(NY)], axis=1)
        t = dot(gbuf[q], part, ((1,), (1,)))
        for i, h in enumerate(halves):
            if q == 0:
                spart[h] = t[:, i * 128:(i + 1) * 128]
            else:
                spart[h] += t[:, i * 128:(i + 1) * 128]
            if q == NQ - 1:
                start(spart.at[h, rows(other, half)], crecv.at[h], cs.at[h], cr.at[h], dev(0, 0, 0, 1))

    for u in range(len(units)):
        gather_y(*units[u])
        if u >= 5:
            gather_pair(*units[u - 5])
    for u in (3, 4, 5):
        gather_pair(*units[u])
    score_term(0, (0, 1))
    score_term(1, (0, 1))
    score_term(2, (0,))
    score_term(3, (0,))
    score_term(2, (1,))
    score_term(3, (1,))
    for h in range(2):
        wait(crecv.at[h], cr.at[h])
        crecv[h] = crecv[h] + spart[h, rows(c, half)]
        xsend[h] = encode_wide(crecv[h])
        for dx in (2, 1, 3):
            to = lax.rem(x + dx, NX)
            start(xsend.at[h, rows(to, chunk)], xrecv.at[h, dx - 1], xs.at[h], xr.at[h], dev(0, 0, dx, 0))
    mine = c * NX + x
    r = []
    for h in range(2):
        wait(xrecv.at[h], xr.at[h])
        s = crecv[h, rows(x, chunk)]
        for i in range(NX - 1):
            s = s + decode_wide(xrecv[h, i])
        r.append(s * scale)
    r = jnp.concatenate(r, axis=1)
    sall[rows(mine, chunk)] = r
    gp[...] = dot(r, r, ((0,), (0,)), precision=lax.Precision.HIGHEST) * (1.0 / total)

    def each_core(core, body):
        @pl.when(core == 0)
        def _():
            body(slice(None))

        @pl.when(core == 1)
        def _():
            body(pl.ds(128, 128))

    spot = (c * NX + x) * NY + y
    for core in range(NC):
        @pl.when(c == core)
        def _():
            for i, (dy, dx, dc) in enumerate(plane):
                lanes = pl.ds(128, 128) if (core + dc) % NC else slice(None)
                to = ((core + dc) % NC * NX + lax.rem(x + dx, NX)) * NY + lax.rem(y + dy, NY)
                start(
                    gp.at[rows(to, 8), lanes], gprecv.at[i, :, lanes],
                    ps.at[2], pr.at[2], dev(0, dy, dx, dc),
                )

    def sum_plane(lanes):
        wait(gprecv.at[:, :, lanes], pr.at[2])
        s = gp[rows(spot, 8), lanes]
        for i in range(len(plane)):
            s = s + gprecv[i, :, lanes]
        gzall[z, :, lanes] = s
        for dz in far:
            own = gzall.at[z, :, lanes]
            start(own, own, ps.at[6], pr.at[6], dev(dz, 0, 0, 0))

    each_core(c, sum_plane)
    for dx in (2, 1, 3):
        own = sall.at[rows(mine, chunk)]
        start(own, own, ps.at[4], pr.at[4], dev(0, 0, dx, 0))

    def sum_z(lanes):
        wait(gzall.at[pl.ds(0, NZ - 1), :, lanes], pr.at[6])
        s = gzall[0, :, lanes]
        for i in range(1, NZ):
            s = s + gzall[i, :, lanes]
        own = gram_ref.at[rows(spot, 8), lanes]
        own[...] = s
        for p in plane:
            start(own, own, ps.at[8], pr.at[8], dev(0, *p))

    each_core(c, sum_z)
    gram_ref[128:, :128] = jnp.zeros((128, 128), F32)
    wait(sall.at[pl.ds(0, 3 * chunk)], pr.at[4])
    own = sall.at[rows(c, half)]
    start(own, own, ps.at[7], pr.at[7], dev(0, 0, 0, 1))
    out1 = pltpu.make_async_copy(own, scores_ref.at[rows(c, half)], out_sem.at[0])
    out1.start()
    wait(sall.at[pl.ds(0, half)], pr.at[7])
    own = sall.at[rows(other, half)]
    out2 = pltpu.make_async_copy(own, scores_ref.at[rows(other, half)], out_sem.at[1])
    out2.start()
    out1.wait()
    out2.wait()

    @pl.when(c == 0)
    def _():
        wait(spart.at[0, pl.ds(0, 368)], pr.at[8])

    @pl.when(c == 1)
    def _():
        wait(spart.at[0, pl.ds(0, 376)], pr.at[8])

    for q in range(NQ):
        wait(psend.at[q], ks.at[q])
        wait(ysend.at[q], ys.at[q])
        wait(ysend.at[q], us.at[q])
        wait(psend.at[q], ws.at[q])

        @pl.when(lax.rem(pair + q, 2) == 0)
        def _():
            wait(lall.at[q, 0, pl.ds(0, 96)], zs.at[q])
            wait(zrecv.at[q], ls.at[q])

        @pl.when(lax.rem(pair + q, 2) == 1)
        def _():
            wait(lall.at[q, 0, pl.ds(0, 128)], zs.at[q])

    for h in range(2):
        wait(crecv.at[h], cs.at[h])
        wait(xrecv.at[h], xs.at[h])
    wait(sall.at[pl.ds(0, 3 * chunk)], ps.at[4])
    wait(sall.at[pl.ds(0, half)], ps.at[7])

    def sent(lanes):
        wait(gzall.at[pl.ds(0, NZ - 1), :, lanes], ps.at[6])
        wait(gprecv.at[:, :, lanes], ps.at[8])

    each_core(c, sent)

    @pl.when(c == 0)
    def _():
        wait(spart.at[0, pl.ds(0, 368)], ps.at[2])

    @pl.when(c == 1)
    def _():
        wait(spart.at[0, pl.ds(0, 376)], ps.at[2])


def scores_and_gram(genotypes, basis_in):
    n, v = genotypes.shape
    k = basis_in.shape[1]
    total_samples = n * lax.axis_size("samples")
    scale = 1.0 / (v * lax.axis_size("variants")) ** 0.5
    part = v // NQ
    chunk = n // (NC * NX)
    dma = pltpu.SemaphoreType.DMA
    vmem = pl.BlockSpec(memory_space=pltpu.VMEM)
    return pl.pallas_call(
        functools.partial(comm_kernel, scale, total_samples),
        out_shape=[jax.ShapeDtypeStruct((n, k), F32), jax.ShapeDtypeStruct((k, k), F32)],
        in_specs=[pl.BlockSpec(memory_space=pl.ANY)] * 2,
        out_specs=[pl.BlockSpec(memory_space=pl.ANY), vmem],
        scratch_shapes=[
            pltpu.VMEM((n, k), BF16),
            pltpu.VMEM((NQ, n, part), BF16),
            pltpu.VMEM((NQ, NY, k, 128), F32),
            pltpu.VMEM((NQ, 2, NY, k // 4, 128), BF16),
            pltpu.VMEM((NQ, 2, NY, k // 4, 128), BF16),
            pltpu.VMEM((NQ, 2, NY - 1, k // 4, 128), BF16),
            pltpu.VMEM((NQ, 2, NY - 1, k // 4, 128), BF16),
            pltpu.VMEM((NQ, 2, k // 4, 128), F32),
            pltpu.VMEM((NQ, 2, k // 4, 128), BF16),
            pltpu.VMEM((NQ, 2, 7 * 16, 128), BF16),
            pltpu.VMEM((NQ, NY, k, 128), BF16),
            pltpu.VMEM((2, n, k // 2), F32),
            pltpu.VMEM((2, n // NC, k // 2), F32),
            pltpu.VMEM((2, n // NC, k // 2), BF16),
            pltpu.VMEM((2, NX - 1, chunk, k // 2), BF16),
            pltpu.VMEM((n, k), F32),
            pltpu.VMEM((k, k), F32),
            pltpu.VMEM((NX * NY * NC - 1, 8, k), F32),
            pltpu.VMEM((NZ, 8, k), F32),
            dma((NQ + 1,)), dma((2,)), pltpu.SemaphoreType.REGULAR((3,)),
            dma((NQ,)), dma((NQ, 2)), dma((NQ,)), dma((NQ, 2)), dma((NQ,)), dma((NQ, 2)),
            dma((NQ,)), dma((NQ, 2)), dma((NQ,)), dma((NQ, 2)), dma((NQ,)), dma((NQ, 2)),
            dma((2,)), dma((2,)), dma((2,)), dma((2,)),
            dma((9,)), dma((9,)),
        ],
        compiler_params=pltpu.CompilerParams(
            collective_id=0, has_side_effects=True, vmem_limit_bytes=24 << 20
        ),
        cost_estimate=pl.CostEstimate(flops=4 * n * v * k, bytes_accessed=2 * n * v, transcendentals=0),
        name="scores_and_gram",
    )(*(pltpu.with_memory_space_constraint(a, pltpu.HBM) for a in (genotypes, basis_in)))


def eliminate(a, panel):
    n = a.shape[0]
    row, col = (lax.broadcasted_iota(jnp.int32, (n, n), i) for i in (0, 1))
    eye = jnp.where(row == col, 1.0, 0.0)
    sub = lax.broadcasted_iota(jnp.int32, (8, n), 0)
    left = [a[8 * i:8 * i + 8] for i in range(n // 8)]
    right = [eye[8 * i:8 * i + 8] for i in range(n // 8)]
    upper, inverse = [], []
    for j0 in range(0, n, panel):
        lo = j0 // 8
        cols = [
            [jnp.broadcast_to(g[:, j0 + k:j0 + k + 1], (8, n)) for g in left[lo:]]
            for k in range(panel)
        ]
        for k in range(panel):
            j = j0 + k
            v, s = j // 8, j % 8
            pivot = cols[k][v - lo][s:s + 1]
            inv = 1.0 / pivot
            root = lax.rsqrt(pivot)
            ra, rb = left[v][s:s + 1], right[v][s:s + 1]
            upper.append(ra * root)
            inverse.append(rb * root)
            if j == n - 1:
                break
            sa = jnp.broadcast_to(ra * inv, (8, n))
            sb = jnp.broadcast_to(rb * inv, (8, n))
            sc = [jnp.broadcast_to(cols[m][v - lo][s:s + 1] * inv, (8, n)) for m in range(k + 1, panel)]
            for i in range(v if s < 7 else v + 1, n // 8):
                c = cols[k][i - lo]
                if i == v:
                    c = jnp.where(sub > s, c, 0.0)
                left[i] = left[i] - c * sa
                right[i] = right[i] - c * sb
                for m in range(k + 1, panel):
                    cols[m][i - lo] = cols[m][i - lo] - c * sc[m - k - 1]
    upper = jnp.where(row <= col, jnp.concatenate(upper, axis=0), 0.0)
    inverse = jnp.where(row >= col, jnp.concatenate(inverse, axis=0), 0.0)
    return upper, inverse


def split(a):
    high = a.astype(BF16)
    return high, (a - high.astype(F32)).astype(BF16)


def dot3(a, b, dims):
    (ah, al), (bh, bl) = split(a), split(b)
    return dot(ah, bh, dims) + (dot(ah, bl, dims) + dot(al, bh, dims))


def factor_kernel(panel, gram, scores_hbm, basis_hbm, factor, scores, basis, sems):
    n = gram.shape[0]
    h = n // 2
    load = pltpu.make_async_copy(scores_hbm, scores, sems.at[0])
    load.start()
    u11, v1 = eliminate(gram[:h, :h], panel)
    load.wait()
    u12 = dot(v1, gram[:h, h:], ((1,), (0,)), precision=lax.Precision.HIGHEST)
    a22 = gram[h:, h:] - dot(u12, u12, ((0,), (0,)), precision=lax.Precision.HIGHEST)
    first = dot3(scores[:, :h], v1, ((1,), (1,)))
    rest = scores[:, h:] - dot3(first, u12, ((1,), (0,)))
    u22, v2 = eliminate(a22, panel)
    basis[0] = first
    basis[1] = dot3(rest, v2, ((1,), (1,)))
    out1 = pltpu.make_async_copy(basis.at[0], basis_hbm.at[:, pl.ds(0, h)], sems.at[1])
    out1.start()
    out2 = pltpu.make_async_copy(basis.at[1], basis_hbm.at[:, pl.ds(h, h)], sems.at[2])
    out2.start()
    factor[:h, :h] = u11
    factor[:h, h:] = u12
    factor[h:, :h] = jnp.zeros((h, h), F32)
    factor[h:, h:] = u22
    out1.wait()
    out2.wait()


def factor_and_basis(gram, scores):
    n, k = scores.shape
    vmem, hbm = pl.BlockSpec(memory_space=pltpu.VMEM), pl.BlockSpec(memory_space=pltpu.HBM)
    return pl.pallas_call(
        functools.partial(factor_kernel, 8),
        out_shape=[jax.ShapeDtypeStruct(scores.shape, F32), jax.ShapeDtypeStruct(gram.shape, F32)],
        in_specs=[vmem, hbm],
        out_specs=[hbm, vmem],
        scratch_shapes=[
            pltpu.VMEM((n, k), F32),
            pltpu.VMEM((2, n, k // 2), F32),
            pltpu.SemaphoreType.DMA((3,)),
        ],
        compiler_params=pltpu.CompilerParams(vmem_limit_bytes=40 << 20),
        name="factor_and_basis",
    )(gram, scores)


def local(genotypes, basis_in):
    scores, gram = scores_and_gram(genotypes, basis_in)
    return tuple(factor_and_basis(gram, scores))


def solution(mesh):
    placed = (P("samples", "variants"), P("samples", None))
    return jax.shard_map(
        local, mesh=mesh, in_specs=placed, out_specs=(P("samples", None), P()), check_vma=False
    )
```

```python
import functools

import jax
import jax.numpy as jnp
from jax import lax
from jax.experimental import pallas as pl
from jax.experimental.pallas import tpu as pltpu
from jax.sharding import PartitionSpec as P

MESH = pl.DeviceIdType.MESH
NZ, NY, NX, NC = 16, 4, 4, 2
NQ = 4
LATE = 5
F32, BF16 = jnp.float32, jnp.bfloat16
SHIFT = 4096.0
LOG_SHIFT = 8.317766166719343
WIDE_SHIFT = 16384.0
LOG_WIDE_SHIFT = 9.704060527839234


def encode(x):
    s = x * SHIFT
    s2 = s * s
    return (s2 * s2 * s).astype(BF16)


def decode(y):
    y = y.astype(F32)
    r = jnp.exp(jnp.log(jnp.abs(y)) * 0.2 - LOG_SHIFT)
    return jnp.where(y < 0, -r, r)


def encode_wide(x):
    s = x * WIDE_SHIFT
    return (s * s * s).astype(BF16)


def decode_wide(y):
    y = y.astype(F32)
    r = jnp.exp(jnp.log(jnp.abs(y)) * (1.0 / 3.0) - LOG_WIDE_SHIFT)
    return jnp.where(y < 0, -r, r)


def hops(d, n):
    return min(d, n - d)


def dot(a, b, dims, **kw):
    return lax.dot_general(a, b, (dims, ((), ())), preferred_element_type=F32, **kw)


def comm_kernel(
    scale, total, g_hbm, b_hbm, scores_ref, gram_ref,
    bbuf, gbuf, tf, psend, precv, ysend, yrecv, sf, zsend, zrecv, lall,
    spart, crecv, xsend, xrecv, sall, gp, gprecv, gzall,
    load_sem, out_sem, known, ks, kr, ys, yr, zs, zr, ls, lr, us, ur, ws, wr, cs, cr, xs, xr, ps, pr,
):
    samp, var = lax.axis_index("samples"), lax.axis_index("variants")
    z, y = lax.div(samp, NY), lax.rem(samp, NY)
    x, c = lax.div(var, NC), lax.rem(var, NC)
    pair = lax.div(z, 2)

    def dev(dz, dy, dx, dc):
        return (
            lax.rem(z + dz, NZ) * NY + lax.rem(y + dy, NY),
            lax.rem(x + dx, NX) * NC + lax.rem(c + dc, NC),
        )

    def start(src, dst, send, recv, to):
        pltpu.make_async_remote_copy(
            src_ref=src, dst_ref=dst, send_sem=send, recv_sem=recv,
            device_id=to, device_id_type=MESH,
        ).start()

    def wait(ref, sem):
        pltpu.make_async_copy(ref, ref, sem).wait()

    def signal(sem, to):
        pl.semaphore_signal(sem, inc=1, device_id=to, device_id_type=MESH)

    def rows(i, n):
        return pl.ds(pl.multiple_of(i * n, n), n)

    plane = [(dy, dx, dc) for dy in range(NY) for dx in range(NX) for dc in range(NC)][1:]
    plane.sort(key=lambda p: -hops(p[0], NY) - hops(p[1], NX))
    far = sorted(range(1, NZ), key=lambda d: -hops(d, NZ))
    near = [(dz, 0, 0, 0) for dz in (2, 14, 1, 15)] + [(0, dy, 0, 0) for dy in (2, 1, 3)]
    near += [(0, 0, dx, 0) for dx in (2, 1, 3)] + [(0, 0, 0, 1)]

    load_b = pltpu.make_async_copy(b_hbm, bbuf, load_sem.at[NQ])
    load_b.start()
    cols = gbuf.shape[2]
    loads = [
        pltpu.make_async_copy(g_hbm.at[:, pl.ds(q * cols, cols)], gbuf.at[q], load_sem.at[q])
        for q in range(NQ)
    ]
    for load in loads:
        load.start()
    barrier = pltpu.get_barrier_semaphore()
    for p in near:
        signal(barrier, dev(*p))

    def term(q):
        loads[q].wait()
        t = dot(bbuf[...], gbuf[q], ((0,), (0,)))
        for i in range(NY):
            tf[q, i] = t[:, i * 128:(i + 1) * 128]

    units = [(q, h) for q in range(NQ) for h in range(2)]

    def parity(h):
        return lax.rem(z + h, 2)

    def partner(h, dy=0):
        return dev(1 + 14 * parity(h), dy, 0, 0)

    def keep(h):
        return rows(2 * h + parity(h), 64)

    def send_pair(q):
        for h in range(2):
            for i in range(NY):
                psend[q, h, i] = encode(tf[q, i, rows(2 * h + 1 - parity(h), 64)])
            start(psend.at[q, h], precv.at[q, h], ks.at[q], kr.at[q, h], partner(h))

    def send_y(q, h):
        wait(precv.at[q, h], kr.at[q, h])
        for dy in (2, 1, 3, 0):
            to = lax.rem(y + dy, NY)
            s = tf[q, to, keep(h)] + decode(precv[q, h, to])
            if dy == 0:
                sf[q, h] = s
                continue
            ysend[q, h, dy - 1] = encode(s)
            start(ysend.at[q, h, dy - 1], yrecv.at[q, h, dy - 1], ys.at[q], yr.at[q, h], dev(0, dy, 0, 0))

    def send_z(q, h):
        wait(yrecv.at[q, h], yr.at[q, h])
        s = sf[q, h]
        for i in range(NY - 1):
            s = s + decode(yrecv[q, h, i])
        sf[q, h] = s
        zsend[q, h] = encode(s)
        shift = lax.rem(pair + q, 2)
        for i in (2, 1, 3, 0):
            def send_tile(i=i):
                d = 2 * i + shift
                to = lax.div(lax.rem(pair + d, 8), 2)
                start(
                    zsend.at[q, h, rows(to, 16)], zrecv.at[q, h, rows(d - 1, 16)],
                    zs.at[q], zr.at[q, h], dev(2 * d, 0, 0, 0),
                )
            if i:
                send_tile()
            else:
                pl.when(shift == 1)(send_tile)

    def finish_tile(q, h):
        @pl.when(lax.rem(pair + q, 2) == 0)
        def _():
            wait(zrecv.at[q, h], zr.at[q, h])
            s = sf[q, h, rows(lax.div(pair, 2), 16)]
            for i in range(7):
                s = s + decode(zrecv[q, h, i * 16:(i + 1) * 16])
            tile = rows(8 * h + 4 * parity(h) + lax.div(pair, 2), 16)
            lall[q, y, tile] = s.astype(BF16)
            for d in (4, 3, 5, 2, 6, 1, 7):
                mine = lall.at[q, y, tile]
                start(mine, mine, ls.at[q], lr.at[q, h], dev(2 * d, 0, 0, 0))

    def gather_y(q, h):
        @pl.when(lax.rem(pair + q, 2) == 0)
        def _():
            wait(lall.at[q, y, pl.ds(0, 48)], lr.at[q, h])

        @pl.when(lax.rem(pair + q, 2) == 1)
        def _():
            wait(lall.at[q, y, pl.ds(0, 64)], lr.at[q, h])

        mine = lall.at[q, y, keep(h)]
        if q == NQ - 1:
            for dy in (2, 1, 3, 0):
                start(mine, mine, ws.at[q], wr.at[q, h], partner(h, dy))
        for dy in (2, 1, 3):
            start(mine, mine, us.at[q], ur.at[q, h], dev(0, dy, 0, 0))

    def gather_pair(q, h):
        wait(yrecv.at[q, h], ur.at[q, h])
        mine = lall.at[q, :, keep(h)]
        start(mine, mine, ws.at[q], wr.at[q, h], partner(h))

    load_b.wait()
    term(0)
    pl.semaphore_wait(barrier, len(near))
    for dz in (2, 14):
        signal(known.at[0], dev(dz, 0, 0, 0))
    send_pair(0)
    term(1)
    send_pair(1)
    pl.semaphore_wait(known.at[0], 2)
    for dz in (4, 12):
        signal(known.at[1], dev(dz, 0, 0, 0))
    for q in range(2, NQ):
        term(q)
        send_pair(q)
    for u in range(len(units) + LATE):
        if u < len(units):
            send_y(*units[u])
        if u == LATE:
            pl.semaphore_wait(known.at[1], 2)
        if u >= LATE:
            send_z(*units[u - LATE])
    for u in units:
        finish_tile(*u)
    half, chunk = spart.shape[1] // NC, spart.shape[1] // (NC * NX)
    other = lax.rem(c + 1, NC)

    def score_term(q, halves):
        for h in halves:
            if q == NQ - 1:
                wait(yrecv.at[q, h], ur.at[q, h])
            wait(precv.at[q, h], wr.at[q, h])
        lo, hi = 128 * halves[0], 128 * (halves[-1] + 1)
        part = jnp.concatenate([lall[q, i, lo:hi] for i in range(NY)], axis=1)
        t = dot(gbuf[q], part, ((1,), (1,)))
        for i, h in enumerate(halves):
            if q == 0:
                spart[h] = t[:, i * 128:(i + 1) * 128]
            else:
                spart[h] += t[:, i * 128:(i + 1) * 128]
            if q == NQ - 1:
                start(spart.at[h, rows(other, half)], crecv.at[h], cs.at[h], cr.at[h], dev(0, 0, 0, 1))

    queue = [u for u in units if u[0] != NQ - 1]
    for i, u in enumerate(units):
        gather_y(*u)
        if i >= LATE and queue:
            gather_pair(*queue.pop(0))
    for u in queue:
        gather_pair(*u)
    score_term(0, (0, 1))
    score_term(1, (0, 1))
    score_term(2, (0,))
    score_term(3, (0,))
    score_term(2, (1,))
    score_term(3, (1,))
    for h in range(2):
        wait(crecv.at[h], cr.at[h])
        crecv[h] = crecv[h] + spart[h, rows(c, half)]
        xsend[h] = encode_wide(crecv[h])
        for dx in (2, 1, 3):
            to = lax.rem(x + dx, NX)
            start(xsend.at[h, rows(to, chunk)], xrecv.at[h, dx - 1], xs.at[h], xr.at[h], dev(0, 0, dx, 0))
    mine = c * NX + x
    r = []
    for h in range(2):
        wait(xrecv.at[h], xr.at[h])
        s = crecv[h, rows(x, chunk)]
        for i in range(NX - 1):
            s = s + decode_wide(xrecv[h, i])
        r.append(s * scale)
    r = jnp.concatenate(r, axis=1)
    sall[rows(mine, chunk)] = r
    gp[...] = dot(r, r, ((0,), (0,)), precision=lax.Precision.HIGHEST) * (1.0 / total)

    def each_core(core, body):
        @pl.when(core == 0)
        def _():
            body(slice(None))

        @pl.when(core == 1)
        def _():
            body(pl.ds(128, 128))

    spot = (c * NX + x) * NY + y
    for core in range(NC):
        @pl.when(c == core)
        def _():
            for i, (dy, dx, dc) in enumerate(plane):
                lanes = pl.ds(128, 128) if (core + dc) % NC else slice(None)
                to = ((core + dc) % NC * NX + lax.rem(x + dx, NX)) * NY + lax.rem(y + dy, NY)
                start(
                    gp.at[rows(to, 8), lanes], gprecv.at[i, :, lanes],
                    ps.at[2], pr.at[2], dev(0, dy, dx, dc),
                )

    def sum_plane(lanes):
        wait(gprecv.at[:, :, lanes], pr.at[2])
        s = gp[rows(spot, 8), lanes]
        for i in range(len(plane)):
            s = s + gprecv[i, :, lanes]
        gzall[z, :, lanes] = s
        for dz in far:
            own = gzall.at[z, :, lanes]
            start(own, own, ps.at[6], pr.at[6], dev(dz, 0, 0, 0))

    each_core(c, sum_plane)
    for dx in (2, 1, 3):
        own = sall.at[rows(mine, chunk)]
        start(own, own, ps.at[4], pr.at[4], dev(0, 0, dx, 0))

    def sum_z(lanes):
        wait(gzall.at[pl.ds(0, NZ - 1), :, lanes], pr.at[6])
        s = gzall[0, :, lanes]
        for i in range(1, NZ):
            s = s + gzall[i, :, lanes]
        own = gram_ref.at[rows(spot, 8), lanes]
        own[...] = s
        for p in plane:
            start(own, own, ps.at[8], pr.at[8], dev(0, *p))

    for q in range(NQ):
        wait(psend.at[q], ks.at[q])
        wait(ysend.at[q], ys.at[q])
        wait(ysend.at[q], us.at[q])
        wait(psend.at[q], ws.at[q])

        @pl.when(lax.rem(pair + q, 2) == 0)
        def _():
            wait(lall.at[q, 0, pl.ds(0, 96)], zs.at[q])
            wait(zrecv.at[q], ls.at[q])

        @pl.when(lax.rem(pair + q, 2) == 1)
        def _():
            wait(lall.at[q, 0, pl.ds(0, 128)], zs.at[q])

    for h in range(2):
        wait(crecv.at[h], cs.at[h])
        wait(xrecv.at[h], xs.at[h])
    each_core(c, sum_z)
    gram_ref[128:, :128] = jnp.zeros((128, 128), F32)
    wait(sall.at[pl.ds(0, 3 * chunk)], pr.at[4])
    own = sall.at[rows(c, half)]
    start(own, own, ps.at[7], pr.at[7], dev(0, 0, 0, 1))
    out1 = pltpu.make_async_copy(own, scores_ref.at[rows(c, half)], out_sem.at[0])
    out1.start()
    wait(sall.at[pl.ds(0, half)], pr.at[7])
    own = sall.at[rows(other, half)]
    out2 = pltpu.make_async_copy(own, scores_ref.at[rows(other, half)], out_sem.at[1])
    out2.start()
    out1.wait()
    out2.wait()

    @pl.when(c == 0)
    def _():
        wait(spart.at[0, pl.ds(0, 368)], pr.at[8])

    @pl.when(c == 1)
    def _():
        wait(spart.at[0, pl.ds(0, 376)], pr.at[8])

    wait(sall.at[pl.ds(0, 3 * chunk)], ps.at[4])
    wait(sall.at[pl.ds(0, half)], ps.at[7])

    def sent(lanes):
        wait(gzall.at[pl.ds(0, NZ - 1), :, lanes], ps.at[6])
        wait(gprecv.at[:, :, lanes], ps.at[8])

    each_core(c, sent)

    @pl.when(c == 0)
    def _():
        wait(spart.at[0, pl.ds(0, 368)], ps.at[2])

    @pl.when(c == 1)
    def _():
        wait(spart.at[0, pl.ds(0, 376)], ps.at[2])


def scores_and_gram(genotypes, basis_in):
    n, v = genotypes.shape
    k = basis_in.shape[1]
    total_samples = n * lax.axis_size("samples")
    scale = 1.0 / (v * lax.axis_size("variants")) ** 0.5
    part = v // NQ
    chunk = n // (NC * NX)
    dma = pltpu.SemaphoreType.DMA
    vmem = pl.BlockSpec(memory_space=pltpu.VMEM)
    return pl.pallas_call(
        functools.partial(comm_kernel, scale, total_samples),
        out_shape=[jax.ShapeDtypeStruct((n, k), F32), jax.ShapeDtypeStruct((k, k), F32)],
        in_specs=[pl.BlockSpec(memory_space=pl.ANY)] * 2,
        out_specs=[pl.BlockSpec(memory_space=pl.ANY), vmem],
        scratch_shapes=[
            pltpu.VMEM((n, k), BF16),
            pltpu.VMEM((NQ, n, part), BF16),
            pltpu.VMEM((NQ, NY, k, 128), F32),
            pltpu.VMEM((NQ, 2, NY, k // 4, 128), BF16),
            pltpu.VMEM((NQ, 2, NY, k // 4, 128), BF16),
            pltpu.VMEM((NQ, 2, NY - 1, k // 4, 128), BF16),
            pltpu.VMEM((NQ, 2, NY - 1, k // 4, 128), BF16),
            pltpu.VMEM((NQ, 2, k // 4, 128), F32),
            pltpu.VMEM((NQ, 2, k // 4, 128), BF16),
            pltpu.VMEM((NQ, 2, 7 * 16, 128), BF16),
            pltpu.VMEM((NQ, NY, k, 128), BF16),
            pltpu.VMEM((2, n, k // 2), F32),
            pltpu.VMEM((2, n // NC, k // 2), F32),
            pltpu.VMEM((2, n // NC, k // 2), BF16),
            pltpu.VMEM((2, NX - 1, chunk, k // 2), BF16),
            pltpu.VMEM((n, k), F32),
            pltpu.VMEM((k, k), F32),
            pltpu.VMEM((NX * NY * NC - 1, 8, k), F32),
            pltpu.VMEM((NZ, 8, k), F32),
            dma((NQ + 1,)), dma((2,)), pltpu.SemaphoreType.REGULAR((2,)),
            dma((NQ,)), dma((NQ, 2)), dma((NQ,)), dma((NQ, 2)), dma((NQ,)), dma((NQ, 2)),
            dma((NQ,)), dma((NQ, 2)), dma((NQ,)), dma((NQ, 2)), dma((NQ,)), dma((NQ, 2)),
            dma((2,)), dma((2,)), dma((2,)), dma((2,)),
            dma((9,)), dma((9,)),
        ],
        compiler_params=pltpu.CompilerParams(
            collective_id=0, has_side_effects=True, vmem_limit_bytes=24 << 20
        ),
        cost_estimate=pl.CostEstimate(flops=4 * n * v * k, bytes_accessed=2 * n * v, transcendentals=0),
        name="scores_and_gram",
    )(*(pltpu.with_memory_space_constraint(a, pltpu.HBM) for a in (genotypes, basis_in)))


def eliminate(a, panel):
    n = a.shape[0]
    row, col = (lax.broadcasted_iota(jnp.int32, (n, n), i) for i in (0, 1))
    eye = jnp.where(row == col, 1.0, 0.0)
    sub = lax.broadcasted_iota(jnp.int32, (8, n), 0)
    left = [a[8 * i:8 * i + 8] for i in range(n // 8)]
    right = [eye[8 * i:8 * i + 8] for i in range(n // 8)]
    upper, inverse = [], []
    for j0 in range(0, n, panel):
        lo = j0 // 8
        cols = [
            [jnp.broadcast_to(g[:, j0 + k:j0 + k + 1], (8, n)) for g in left[lo:]]
            for k in range(panel)
        ]
        for k in range(panel):
            j = j0 + k
            v, s = j // 8, j % 8
            pivot = cols[k][v - lo][s:s + 1]
            inv = 1.0 / pivot
            root = lax.rsqrt(pivot)
            ra, rb = left[v][s:s + 1], right[v][s:s + 1]
            upper.append(ra * root)
            inverse.append(rb * root)
            if j == n - 1:
                break
            sa = jnp.broadcast_to(ra * inv, (8, n))
            sb = jnp.broadcast_to(rb * inv, (8, n))
            sc = [jnp.broadcast_to(cols[m][v - lo][s:s + 1] * inv, (8, n)) for m in range(k + 1, panel)]
            for i in range(v if s < 7 else v + 1, n // 8):
                c = cols[k][i - lo]
                if i == v:
                    c = jnp.where(sub > s, c, 0.0)
                left[i] = left[i] - c * sa
                right[i] = right[i] - c * sb
                for m in range(k + 1, panel):
                    cols[m][i - lo] = cols[m][i - lo] - c * sc[m - k - 1]
    upper = jnp.where(row <= col, jnp.concatenate(upper, axis=0), 0.0)
    inverse = jnp.where(row >= col, jnp.concatenate(inverse, axis=0), 0.0)
    return upper, inverse


def split(a):
    high = a.astype(BF16)
    return high, (a - high.astype(F32)).astype(BF16)


def dot3(a, b, dims):
    (ah, al), (bh, bl) = split(a), split(b)
    return dot(ah, bh, dims) + (dot(ah, bl, dims) + dot(al, bh, dims))


def factor_kernel(panel, gram, scores_hbm, basis_hbm, factor_hbm, scores, basis, factor, sems):
    n = gram.shape[0]
    h = n // 2
    load = pltpu.make_async_copy(scores_hbm, scores, sems.at[0])
    load.start()
    u11, v1 = eliminate(gram[:h, :h], panel)
    load.wait()
    u12 = dot(v1, gram[:h, h:], ((1,), (0,)), precision=lax.Precision.HIGHEST)
    a22 = gram[h:, h:] - dot(u12, u12, ((0,), (0,)), precision=lax.Precision.HIGHEST)
    first = dot3(scores[:, :h], v1, ((1,), (1,)))
    rest = scores[:, h:] - dot3(first, u12, ((1,), (0,)))
    factor[:h, :h] = u11
    factor[:h, h:] = u12
    factor[h:, :h] = jnp.zeros((h, h), F32)
    basis[0] = first
    u22, v2 = eliminate(a22, panel)
    factor[h:, h:] = u22
    outs = [
        pltpu.make_async_copy(factor, factor_hbm, sems.at[3]),
        pltpu.make_async_copy(basis.at[0], basis_hbm.at[:, pl.ds(0, h)], sems.at[1]),
        pltpu.make_async_copy(basis.at[1], basis_hbm.at[:, pl.ds(h, h)], sems.at[2]),
    ]
    outs[0].start()
    outs[1].start()
    basis[1] = dot3(rest, v2, ((1,), (1,)))
    outs[2].start()
    for out in outs:
        out.wait()


def factor_and_basis(gram, scores):
    n, k = scores.shape
    vmem, hbm = pl.BlockSpec(memory_space=pltpu.VMEM), pl.BlockSpec(memory_space=pltpu.HBM)
    return pl.pallas_call(
        functools.partial(factor_kernel, 8),
        out_shape=[jax.ShapeDtypeStruct(scores.shape, F32), jax.ShapeDtypeStruct(gram.shape, F32)],
        in_specs=[vmem, hbm],
        out_specs=[hbm, hbm],
        scratch_shapes=[
            pltpu.VMEM((n, k), F32),
            pltpu.VMEM((2, n, k // 2), F32),
            pltpu.VMEM((k, k), F32),
            pltpu.SemaphoreType.DMA((4,)),
        ],
        compiler_params=pltpu.CompilerParams(vmem_limit_bytes=40 << 20),
        name="factor_and_basis",
    )(gram, scores)


def local(genotypes, basis_in):
    scores, gram = scores_and_gram(genotypes, basis_in)
    return tuple(factor_and_basis(gram, scores))


def solution(mesh):
    placed = (P("samples", "variants"), P("samples", None))
    return jax.shard_map(
        local, mesh=mesh, in_specs=placed, out_specs=(P("samples", None), P()), check_vma=False
    )
```

```python
import functools

import jax
import jax.numpy as jnp
from jax import lax
from jax.experimental import pallas as pl
from jax.experimental.pallas import tpu as pltpu
from jax.sharding import PartitionSpec as P

MESH = pl.DeviceIdType.MESH
NZ, NY, NX, NC = 16, 4, 4, 2
NQ = 4
LATE = 5
F32, BF16 = jnp.float32, jnp.bfloat16
SHIFT = 4096.0
LOG_SHIFT = 8.317766166719343
WIDE_SHIFT = 16384.0
LOG_WIDE_SHIFT = 9.704060527839234


def encode(x):
    s = x * SHIFT
    s2 = s * s
    return (s2 * s2 * s).astype(BF16)


def decode(y):
    y = y.astype(F32)
    r = jnp.exp(jnp.log(jnp.abs(y)) * 0.2 - LOG_SHIFT)
    return jnp.where(y < 0, -r, r)


def encode_wide(x):
    s = x * WIDE_SHIFT
    return (s * s * s).astype(BF16)


def decode_wide(y):
    y = y.astype(F32)
    r = jnp.exp(jnp.log(jnp.abs(y)) * (1.0 / 3.0) - LOG_WIDE_SHIFT)
    return jnp.where(y < 0, -r, r)


def hops(d, n):
    return min(d, n - d)


def dot(a, b, dims, **kw):
    return lax.dot_general(a, b, (dims, ((), ())), preferred_element_type=F32, **kw)


def comm_kernel(
    scale, total, g_hbm, b_hbm, scores_ref, gram_ref,
    bbuf, gbuf, tf, psend, precv, ysend, yrecv, sf, zsend, zrecv, lall,
    spart, crecv, xsend, xrecv, sall, gp, gprecv, gzall,
    load_sem, out_sem, known, ks, kr, ys, yr, zs, zr, ls, lr, us, ur, ws, wr, cs, cr, xs, xr, ps, pr,
):
    samp, var = lax.axis_index("samples"), lax.axis_index("variants")
    z, y = lax.div(samp, NY), lax.rem(samp, NY)
    x, c = lax.div(var, NC), lax.rem(var, NC)
    pair = lax.div(z, 2)

    def dev(dz, dy, dx, dc):
        return (
            lax.rem(z + dz, NZ) * NY + lax.rem(y + dy, NY),
            lax.rem(x + dx, NX) * NC + lax.rem(c + dc, NC),
        )

    def start(src, dst, send, recv, to):
        pltpu.make_async_remote_copy(
            src_ref=src, dst_ref=dst, send_sem=send, recv_sem=recv,
            device_id=to, device_id_type=MESH,
        ).start()

    def wait(ref, sem):
        pltpu.make_async_copy(ref, ref, sem).wait()

    def signal(sem, to):
        pl.semaphore_signal(sem, inc=1, device_id=to, device_id_type=MESH)

    def rows(i, n):
        return pl.ds(pl.multiple_of(i * n, n), n)

    plane = [(dy, dx, dc) for dy in range(NY) for dx in range(NX) for dc in range(NC)][1:]
    plane.sort(key=lambda p: -hops(p[0], NY) - hops(p[1], NX))
    far = sorted(range(1, NZ), key=lambda d: -hops(d, NZ))
    near = [(dz, 0, 0, 0) for dz in (2, 14, 1, 15)] + [(0, dy, 0, 0) for dy in (2, 1, 3)]
    near += [(0, 0, dx, 0) for dx in (2, 1, 3)] + [(0, 0, 0, 1)]

    load_b = pltpu.make_async_copy(b_hbm, bbuf, load_sem.at[NQ])
    load_b.start()
    cols = gbuf.shape[2]
    loads = [
        pltpu.make_async_copy(g_hbm.at[:, pl.ds(q * cols, cols)], gbuf.at[q], load_sem.at[q])
        for q in range(NQ)
    ]
    for load in loads:
        load.start()
    barrier = pltpu.get_barrier_semaphore()
    for p in near:
        signal(barrier, dev(*p))

    def term(q):
        loads[q].wait()
        t = dot(bbuf[...], gbuf[q], ((0,), (0,)))
        for i in range(NY):
            tf[q, i] = t[:, i * 128:(i + 1) * 128]

    units = [(q, h) for q in range(NQ) for h in range(2)]

    def parity(h):
        return lax.rem(z + h, 2)

    def partner(h, dy=0):
        return dev(1 + 14 * parity(h), dy, 0, 0)

    def keep(h):
        return rows(2 * h + parity(h), 64)

    def send_pair(q):
        for h in range(2):
            for dy in (2, 1, 3, 0):
                to = lax.rem(y + dy, NY)
                psend[q, h, dy] = encode(tf[q, to, rows(2 * h + 1 - parity(h), 64)])
                start(psend.at[q, h, dy], precv.at[q, h, dy], ks.at[q], kr.at[q, h, dy], partner(h))

    def send_y(q, h):
        for dy in (2, 1, 3, 0):
            to = lax.rem(y + dy, NY)
            wait(precv.at[q, h, dy], kr.at[q, h, dy])
            s = tf[q, to, keep(h)] + decode(precv[q, h, dy])
            if dy == 0:
                sf[q, h] = s
                continue
            ysend[q, h, dy - 1] = encode(s)
            start(ysend.at[q, h, dy - 1], yrecv.at[q, h, dy - 1], ys.at[q], yr.at[q, h], dev(0, dy, 0, 0))

    def send_z(q, h):
        wait(yrecv.at[q, h], yr.at[q, h])
        s = sf[q, h]
        for i in range(NY - 1):
            s = s + decode(yrecv[q, h, i])
        sf[q, h] = s
        zsend[q, h] = encode(s)
        shift = lax.rem(pair + q, 2)
        for i in (2, 1, 3, 0):
            def send_tile(i=i):
                d = 2 * i + shift
                to = lax.div(lax.rem(pair + d, 8), 2)
                start(
                    zsend.at[q, h, rows(to, 16)], zrecv.at[q, h, rows(d - 1, 16)],
                    zs.at[q], zr.at[q, h], dev(2 * d, 0, 0, 0),
                )
            if i:
                send_tile()
            else:
                pl.when(shift == 1)(send_tile)

    def finish_tile(q, h):
        @pl.when(lax.rem(pair + q, 2) == 0)
        def _():
            wait(zrecv.at[q, h], zr.at[q, h])
            s = sf[q, h, rows(lax.div(pair, 2), 16)]
            for i in range(7):
                s = s + decode(zrecv[q, h, i * 16:(i + 1) * 16])
            tile = rows(8 * h + 4 * parity(h) + lax.div(pair, 2), 16)
            lall[q, y, tile] = s.astype(BF16)
            for d in (4, 3, 5, 2, 6, 1, 7):
                mine = lall.at[q, y, tile]
                start(mine, mine, ls.at[q], lr.at[q, h], dev(2 * d, 0, 0, 0))

    def gather_y(q, h):
        @pl.when(lax.rem(pair + q, 2) == 0)
        def _():
            wait(lall.at[q, y, pl.ds(0, 48)], lr.at[q, h])

        @pl.when(lax.rem(pair + q, 2) == 1)
        def _():
            wait(lall.at[q, y, pl.ds(0, 64)], lr.at[q, h])

        mine = lall.at[q, y, keep(h)]
        if q == NQ - 1:
            for dy in (2, 1, 3, 0):
                start(mine, mine, ws.at[q], wr.at[q, h], partner(h, dy))
        for dy in (2, 1, 3):
            start(mine, mine, us.at[q], ur.at[q, h], dev(0, dy, 0, 0))

    def gather_pair(q, h):
        wait(yrecv.at[q, h], ur.at[q, h])
        mine = lall.at[q, :, keep(h)]
        start(mine, mine, ws.at[q], wr.at[q, h], partner(h))

    load_b.wait()
    term(0)
    pl.semaphore_wait(barrier, len(near))
    for dz in (2, 14):
        signal(known.at[0], dev(dz, 0, 0, 0))
    send_pair(0)
    for q in range(1, NQ):
        term(q)
        send_pair(q)
        if q == 2:
            pl.semaphore_wait(known.at[0], 2)
            for dz in (4, 12):
                signal(known.at[1], dev(dz, 0, 0, 0))
    for u in range(len(units) + LATE):
        if u < len(units):
            send_y(*units[u])
        if u == LATE:
            pl.semaphore_wait(known.at[1], 2)
        if u >= LATE:
            send_z(*units[u - LATE])
    for u in units:
        finish_tile(*u)
    half, chunk = spart.shape[1] // NC, spart.shape[1] // (NC * NX)
    other = lax.rem(c + 1, NC)

    def score_term(q, halves):
        for h in halves:
            if q == NQ - 1:
                wait(yrecv.at[q, h], ur.at[q, h])
            wait(precv.at[q, h], wr.at[q, h])
        lo, hi = 128 * halves[0], 128 * (halves[-1] + 1)
        part = jnp.concatenate([lall[q, i, lo:hi] for i in range(NY)], axis=1)
        if q == NQ - 1:
            h, = halves
            for core in (other, c):
                spart[h, rows(core, half)] += dot(gbuf[q, rows(core, half)], part, ((1,), (1,)))
                if core is other:
                    start(spart.at[h, rows(other, half)], crecv.at[h], cs.at[h], cr.at[h], dev(0, 0, 0, 1))
            return
        t = dot(gbuf[q], part, ((1,), (1,)))
        for i, h in enumerate(halves):
            if q == 0:
                spart[h] = t[:, i * 128:(i + 1) * 128]
            else:
                spart[h] += t[:, i * 128:(i + 1) * 128]

    queue = [u for u in units if u[0] != NQ - 1]
    for i, u in enumerate(units):
        gather_y(*u)
        if i >= LATE and queue:
            gather_pair(*queue.pop(0))
    for u in queue:
        gather_pair(*u)
    score_term(0, (0, 1))
    score_term(1, (0, 1))
    score_term(2, (0,))
    score_term(3, (0,))
    score_term(2, (1,))
    score_term(3, (1,))
    for h in range(2):
        wait(crecv.at[h], cr.at[h])
        crecv[h] = crecv[h] + spart[h, rows(c, half)]
        xsend[h] = encode_wide(crecv[h])
        for dx in (2, 1, 3):
            to = lax.rem(x + dx, NX)
            start(xsend.at[h, rows(to, chunk)], xrecv.at[h, dx - 1], xs.at[h], xr.at[h], dev(0, 0, dx, 0))
    mine = c * NX + x
    r = []
    for h in range(2):
        wait(xrecv.at[h], xr.at[h])
        s = crecv[h, rows(x, chunk)]
        for i in range(NX - 1):
            s = s + decode_wide(xrecv[h, i])
        r.append(s * scale)
        sall[rows(mine, chunk), h * 128:(h + 1) * 128] = r[h]
        for i in range(h + 1):
            gp[i * 128:(i + 1) * 128, h * 128:(h + 1) * 128] = (
                dot(r[i], r[h], ((0,), (0,)), precision=lax.Precision.HIGHEST) * (1.0 / total)
            )

    def each_core(core, body):
        @pl.when(core == 0)
        def _():
            body(slice(None))

        @pl.when(core == 1)
        def _():
            body(pl.ds(128, 128))

    spot = (c * NX + x) * NY + y
    for core in range(NC):
        @pl.when(c == core)
        def _():
            for i, (dy, dx, dc) in enumerate(plane):
                lanes = pl.ds(128, 128) if (core + dc) % NC else slice(None)
                to = ((core + dc) % NC * NX + lax.rem(x + dx, NX)) * NY + lax.rem(y + dy, NY)
                start(
                    gp.at[rows(to, 8), lanes], gprecv.at[i, :, lanes],
                    ps.at[2], pr.at[2], dev(0, dy, dx, dc),
                )

    def sum_plane(lanes):
        wait(gprecv.at[:, :, lanes], pr.at[2])
        s = gp[rows(spot, 8), lanes]
        for i in range(len(plane)):
            s = s + gprecv[i, :, lanes]
        gzall[z, :, lanes] = s
        for dz in far:
            own = gzall.at[z, :, lanes]
            start(own, own, ps.at[6], pr.at[6], dev(dz, 0, 0, 0))

    each_core(c, sum_plane)
    for dx in (2, 1, 3):
        own = sall.at[rows(mine, chunk)]
        start(own, own, ps.at[4], pr.at[4], dev(0, 0, dx, 0))

    def sum_z(lanes):
        wait(gzall.at[pl.ds(0, NZ - 1), :, lanes], pr.at[6])
        s = gzall[0, :, lanes]
        for i in range(1, NZ):
            s = s + gzall[i, :, lanes]
        own = gram_ref.at[rows(spot, 8), lanes]
        own[...] = s
        for p in plane:
            start(own, own, ps.at[8], pr.at[8], dev(0, *p))

    for q in range(NQ):
        wait(psend.at[q], ks.at[q])
        wait(ysend.at[q], ys.at[q])
        wait(ysend.at[q], us.at[q])
        wait(psend.at[q], ws.at[q])

        @pl.when(lax.rem(pair + q, 2) == 0)
        def _():
            wait(lall.at[q, 0, pl.ds(0, 96)], zs.at[q])
            wait(zrecv.at[q], ls.at[q])

        @pl.when(lax.rem(pair + q, 2) == 1)
        def _():
            wait(lall.at[q, 0, pl.ds(0, 128)], zs.at[q])

    for h in range(2):
        wait(crecv.at[h], cs.at[h])
        wait(xrecv.at[h], xs.at[h])
    each_core(c, sum_z)
    gram_ref[128:, :128] = jnp.zeros((128, 128), F32)
    wait(sall.at[pl.ds(0, 3 * chunk)], pr.at[4])
    own = sall.at[rows(c, half)]
    start(own, own, ps.at[7], pr.at[7], dev(0, 0, 0, 1))
    out1 = pltpu.make_async_copy(own, scores_ref.at[rows(c, half)], out_sem.at[0])
    out1.start()
    wait(sall.at[pl.ds(0, half)], pr.at[7])
    own = sall.at[rows(other, half)]
    out2 = pltpu.make_async_copy(own, scores_ref.at[rows(other, half)], out_sem.at[1])
    out2.start()
    out1.wait()
    out2.wait()

    @pl.when(c == 0)
    def _():
        wait(spart.at[0, pl.ds(0, 368)], pr.at[8])

    @pl.when(c == 1)
    def _():
        wait(spart.at[0, pl.ds(0, 376)], pr.at[8])

    wait(sall.at[pl.ds(0, 3 * chunk)], ps.at[4])
    wait(sall.at[pl.ds(0, half)], ps.at[7])

    def sent(lanes):
        wait(gzall.at[pl.ds(0, NZ - 1), :, lanes], ps.at[6])
        wait(gprecv.at[:, :, lanes], ps.at[8])

    each_core(c, sent)

    @pl.when(c == 0)
    def _():
        wait(spart.at[0, pl.ds(0, 368)], ps.at[2])

    @pl.when(c == 1)
    def _():
        wait(spart.at[0, pl.ds(0, 376)], ps.at[2])


def scores_and_gram(genotypes, basis_in):
    n, v = genotypes.shape
    k = basis_in.shape[1]
    total_samples = n * lax.axis_size("samples")
    scale = 1.0 / (v * lax.axis_size("variants")) ** 0.5
    part = v // NQ
    chunk = n // (NC * NX)
    dma = pltpu.SemaphoreType.DMA
    vmem = pl.BlockSpec(memory_space=pltpu.VMEM)
    return pl.pallas_call(
        functools.partial(comm_kernel, scale, total_samples),
        out_shape=[jax.ShapeDtypeStruct((n, k), F32), jax.ShapeDtypeStruct((k, k), F32)],
        in_specs=[pl.BlockSpec(memory_space=pl.ANY)] * 2,
        out_specs=[pl.BlockSpec(memory_space=pl.ANY), vmem],
        scratch_shapes=[
            pltpu.VMEM((n, k), BF16),
            pltpu.VMEM((NQ, n, part), BF16),
            pltpu.VMEM((NQ, NY, k, 128), F32),
            pltpu.VMEM((NQ, 2, NY, k // 4, 128), BF16),
            pltpu.VMEM((NQ, 2, NY, k // 4, 128), BF16),
            pltpu.VMEM((NQ, 2, NY - 1, k // 4, 128), BF16),
            pltpu.VMEM((NQ, 2, NY - 1, k // 4, 128), BF16),
            pltpu.VMEM((NQ, 2, k // 4, 128), F32),
            pltpu.VMEM((NQ, 2, k // 4, 128), BF16),
            pltpu.VMEM((NQ, 2, 7 * 16, 128), BF16),
            pltpu.VMEM((NQ, NY, k, 128), BF16),
            pltpu.VMEM((2, n, k // 2), F32),
            pltpu.VMEM((2, n // NC, k // 2), F32),
            pltpu.VMEM((2, n // NC, k // 2), BF16),
            pltpu.VMEM((2, NX - 1, chunk, k // 2), BF16),
            pltpu.VMEM((n, k), F32),
            pltpu.VMEM((k, k), F32),
            pltpu.VMEM((NX * NY * NC - 1, 8, k), F32),
            pltpu.VMEM((NZ, 8, k), F32),
            dma((NQ + 1,)), dma((2,)), pltpu.SemaphoreType.REGULAR((2,)),
            dma((NQ,)), dma((NQ, 2, NY)), dma((NQ,)), dma((NQ, 2)), dma((NQ,)), dma((NQ, 2)),
            dma((NQ,)), dma((NQ, 2)), dma((NQ,)), dma((NQ, 2)), dma((NQ,)), dma((NQ, 2)),
            dma((2,)), dma((2,)), dma((2,)), dma((2,)),
            dma((9,)), dma((9,)),
        ],
        compiler_params=pltpu.CompilerParams(
            collective_id=0, has_side_effects=True, vmem_limit_bytes=24 << 20
        ),
        cost_estimate=pl.CostEstimate(flops=4 * n * v * k, bytes_accessed=2 * n * v, transcendentals=0),
        name="scores_and_gram",
    )(*(pltpu.with_memory_space_constraint(a, pltpu.HBM) for a in (genotypes, basis_in)))


def eliminate(a, panel):
    n = a.shape[0]
    row, col = (lax.broadcasted_iota(jnp.int32, (n, n), i) for i in (0, 1))
    eye = jnp.where(row == col, 1.0, 0.0)
    sub = lax.broadcasted_iota(jnp.int32, (8, n), 0)
    left = [a[8 * i:8 * i + 8] for i in range(n // 8)]
    right = [eye[8 * i:8 * i + 8] for i in range(n // 8)]
    upper, inverse = [], []
    for j0 in range(0, n, panel):
        lo = j0 // 8
        cols = [
            [jnp.broadcast_to(g[:, j0 + k:j0 + k + 1], (8, n)) for g in left[lo:]]
            for k in range(panel)
        ]
        for k in range(panel):
            j = j0 + k
            v, s = j // 8, j % 8
            pivot = cols[k][v - lo][s:s + 1]
            inv = 1.0 / pivot
            root = lax.rsqrt(pivot)
            ra, rb = left[v][s:s + 1], right[v][s:s + 1]
            upper.append(ra * root)
            inverse.append(rb * root)
            if j == n - 1:
                break
            sa = jnp.broadcast_to(ra * inv, (8, n))
            sb = jnp.broadcast_to(rb * inv, (8, n))
            sc = [jnp.broadcast_to(cols[m][v - lo][s:s + 1] * inv, (8, n)) for m in range(k + 1, panel)]
            for i in range(v if s < 7 else v + 1, n // 8):
                c = cols[k][i - lo]
                if i == v:
                    c = jnp.where(sub > s, c, 0.0)
                left[i] = left[i] - c * sa
                right[i] = right[i] - c * sb
                for m in range(k + 1, panel):
                    cols[m][i - lo] = cols[m][i - lo] - c * sc[m - k - 1]
    upper = jnp.where(row <= col, jnp.concatenate(upper, axis=0), 0.0)
    inverse = jnp.where(row >= col, jnp.concatenate(inverse, axis=0), 0.0)
    return upper, inverse


def split(a):
    high = a.astype(BF16)
    return high, (a - high.astype(F32)).astype(BF16)


def dot3(a, b, dims):
    (ah, al), (bh, bl) = split(a), split(b)
    return dot(ah, bh, dims) + (dot(ah, bl, dims) + dot(al, bh, dims))


def factor_kernel(panel, gram, scores_hbm, basis_hbm, factor_hbm, scores, basis, factor, sems):
    n = gram.shape[0]
    h = n // 2
    load = pltpu.make_async_copy(scores_hbm, scores, sems.at[0])
    load.start()
    u11, v1 = eliminate(gram[:h, :h], panel)
    load.wait()
    u12 = dot(v1, gram[:h, h:], ((1,), (0,)), precision=lax.Precision.HIGHEST)
    a22 = gram[h:, h:] - dot(u12, u12, ((0,), (0,)), precision=lax.Precision.HIGHEST)
    first = dot3(scores[:, :h], v1, ((1,), (1,)))
    rest = scores[:, h:] - dot3(first, u12, ((1,), (0,)))
    factor[:h, :h] = u11
    factor[:h, h:] = u12
    factor[h:, :h] = jnp.zeros((h, h), F32)
    basis[0] = first
    u22, v2 = eliminate(a22, panel)
    factor[h:, h:] = u22
    outs = [
        pltpu.make_async_copy(factor, factor_hbm, sems.at[3]),
        pltpu.make_async_copy(basis.at[0], basis_hbm.at[:, pl.ds(0, h)], sems.at[1]),
        pltpu.make_async_copy(basis.at[1], basis_hbm.at[:, pl.ds(h, h)], sems.at[2]),
    ]
    outs[0].start()
    outs[1].start()
    basis[1] = dot3(rest, v2, ((1,), (1,)))
    outs[2].start()
    for out in outs:
        out.wait()


def factor_and_basis(gram, scores):
    n, k = scores.shape
    vmem, hbm = pl.BlockSpec(memory_space=pltpu.VMEM), pl.BlockSpec(memory_space=pltpu.HBM)
    return pl.pallas_call(
        functools.partial(factor_kernel, 8),
        out_shape=[jax.ShapeDtypeStruct(scores.shape, F32), jax.ShapeDtypeStruct(gram.shape, F32)],
        in_specs=[vmem, hbm],
        out_specs=[hbm, hbm],
        scratch_shapes=[
            pltpu.VMEM((n, k), F32),
            pltpu.VMEM((2, n, k // 2), F32),
            pltpu.VMEM((k, k), F32),
            pltpu.SemaphoreType.DMA((4,)),
        ],
        compiler_params=pltpu.CompilerParams(vmem_limit_bytes=40 << 20),
        name="factor_and_basis",
    )(gram, scores)


def local(genotypes, basis_in):
    scores, gram = scores_and_gram(genotypes, basis_in)
    return tuple(factor_and_basis(gram, scores))


def solution(mesh):
    placed = (P("samples", "variants"), P("samples", None))
    return jax.shard_map(
        local, mesh=mesh, in_specs=placed, out_specs=(P("samples", None), P()), check_vma=False
    )
```

```python
import functools

import jax
import jax.numpy as jnp
from jax import lax
from jax.experimental import pallas as pl
from jax.experimental.pallas import tpu as pltpu
from jax.sharding import PartitionSpec as P

MESH = pl.DeviceIdType.MESH
NZ, NY, NX, NC = 16, 4, 4, 2
NQ = 4
LATE = 5
F32, BF16 = jnp.float32, jnp.bfloat16
SHIFT = 4096.0
LOG_SHIFT = 8.317766166719343
WIDE_SHIFT = 16384.0
LOG_WIDE_SHIFT = 9.704060527839234


def encode(x):
    s = x * SHIFT
    s2 = s * s
    return (s2 * s2 * s).astype(BF16)


def decode(y):
    y = y.astype(F32)
    r = jnp.exp(jnp.log(jnp.abs(y)) * 0.2 - LOG_SHIFT)
    return jnp.where(y < 0, -r, r)


def encode_wide(x):
    s = x * WIDE_SHIFT
    return (s * s * s).astype(BF16)


def decode_wide(y):
    y = y.astype(F32)
    r = jnp.exp(jnp.log(jnp.abs(y)) * (1.0 / 3.0) - LOG_WIDE_SHIFT)
    return jnp.where(y < 0, -r, r)


def hops(d, n):
    return min(d, n - d)


def dot(a, b, dims, **kw):
    return lax.dot_general(a, b, (dims, ((), ())), preferred_element_type=F32, **kw)


def comm_kernel(
    scale, total, g_hbm, b_hbm, scores_ref, gram_ref,
    bbuf, gbuf, tf, psend, precv, ysend, yrecv, sf, zsend, zrecv, lall,
    spart, crecv, xsend, xrecv, sall, gp, gprecv, gzall,
    load_sem, out_sem, known, ks, kr, ys, yr, zs, zr, ls, lr, us, ur, ws, wr, cs, cr, xs, xr, ps, pr,
):
    samp, var = lax.axis_index("samples"), lax.axis_index("variants")
    z, y = lax.div(samp, NY), lax.rem(samp, NY)
    x, c = lax.div(var, NC), lax.rem(var, NC)
    pair = lax.div(z, 2)

    def dev(dz, dy, dx, dc):
        return (
            lax.rem(z + dz, NZ) * NY + lax.rem(y + dy, NY),
            lax.rem(x + dx, NX) * NC + lax.rem(c + dc, NC),
        )

    def start(src, dst, send, recv, to):
        pltpu.make_async_remote_copy(
            src_ref=src, dst_ref=dst, send_sem=send, recv_sem=recv,
            device_id=to, device_id_type=MESH,
        ).start()

    def wait(ref, sem):
        pltpu.make_async_copy(ref, ref, sem).wait()

    def signal(sem, to):
        pl.semaphore_signal(sem, inc=1, device_id=to, device_id_type=MESH)

    def rows(i, n):
        return pl.ds(pl.multiple_of(i * n, n), n)

    plane = [(dy, dx, dc) for dy in range(NY) for dx in range(NX) for dc in range(NC)][1:]
    plane.sort(key=lambda p: -hops(p[0], NY) - hops(p[1], NX))
    far = sorted(range(1, NZ), key=lambda d: -hops(d, NZ))
    near = [(dz, 0, 0, 0) for dz in (2, 14, 1, 15)] + [(0, dy, 0, 0) for dy in (2, 1, 3)]
    near += [(0, 0, dx, 0) for dx in (2, 1, 3)] + [(0, 0, 0, 1)]

    load_b = pltpu.make_async_copy(b_hbm, bbuf, load_sem.at[NQ])
    load_b.start()
    cols = gbuf.shape[2]
    loads = [
        pltpu.make_async_copy(g_hbm.at[:, pl.ds(q * cols, cols)], gbuf.at[q], load_sem.at[q])
        for q in range(NQ)
    ]
    for load in loads:
        load.start()
    barrier = pltpu.get_barrier_semaphore()
    for p in near:
        signal(barrier, dev(*p))

    def term(q):
        loads[q].wait()
        t = dot(bbuf[...], gbuf[q], ((0,), (0,)))
        for i in range(NY):
            tf[q, i] = t[:, i * 128:(i + 1) * 128]

    units = [(q, h) for q in range(NQ) for h in range(2)]

    def parity(h):
        return lax.rem(z + h, 2)

    def partner(h, dy=0):
        return dev(1 + 14 * parity(h), dy, 0, 0)

    def keep(h):
        return rows(2 * h + parity(h), 64)

    def send_pair(q):
        for h in range(2):
            for dy in (2, 1, 3, 0):
                to = lax.rem(y + dy, NY)
                psend[q, h, dy] = encode(tf[q, to, rows(2 * h + 1 - parity(h), 64)])
                start(psend.at[q, h, dy], precv.at[q, h, dy], ks.at[q], kr.at[q, h, dy], partner(h))

    def send_y(q, h):
        for dy in (2, 1, 3, 0):
            to = lax.rem(y + dy, NY)
            wait(precv.at[q, h, dy], kr.at[q, h, dy])
            s = tf[q, to, keep(h)] + decode(precv[q, h, dy])
            if dy == 0:
                sf[q, h] = s
                continue
            ysend[q, h, dy - 1] = encode(s)
            start(ysend.at[q, h, dy - 1], yrecv.at[q, h, dy - 1], ys.at[q], yr.at[q, h], dev(0, dy, 0, 0))

    def send_z(q, h):
        wait(yrecv.at[q, h], yr.at[q, h])
        s = sf[q, h]
        for i in range(NY - 1):
            s = s + decode(yrecv[q, h, i])
        sf[q, h] = s
        zsend[q, h] = encode(s)
        shift = lax.rem(pair + q, 2)
        for i in (2, 1, 3, 0):
            def send_tile(i=i):
                d = 2 * i + shift
                to = lax.div(lax.rem(pair + d, 8), 2)
                start(
                    zsend.at[q, h, rows(to, 16)], zrecv.at[q, h, rows(d - 1, 16)],
                    zs.at[q], zr.at[q, h], dev(2 * d, 0, 0, 0),
                )
            if i:
                send_tile()
            else:
                pl.when(shift == 1)(send_tile)

    def finish_tile(q, h):
        @pl.when(lax.rem(pair + q, 2) == 0)
        def _():
            wait(zrecv.at[q, h], zr.at[q, h])
            s = sf[q, h, rows(lax.div(pair, 2), 16)]
            for i in range(7):
                s = s + decode(zrecv[q, h, i * 16:(i + 1) * 16])
            tile = rows(8 * h + 4 * parity(h) + lax.div(pair, 2), 16)
            lall[q, y, tile] = s.astype(BF16)
            for d in (4, 3, 5, 2, 6, 1, 7):
                mine = lall.at[q, y, tile]
                start(mine, mine, ls.at[q], lr.at[q, h], dev(2 * d, 0, 0, 0))

    def gather_y(q, h):
        @pl.when(lax.rem(pair + q, 2) == 0)
        def _():
            wait(lall.at[q, y, pl.ds(0, 48)], lr.at[q, h])

        @pl.when(lax.rem(pair + q, 2) == 1)
        def _():
            wait(lall.at[q, y, pl.ds(0, 64)], lr.at[q, h])

        mine = lall.at[q, y, keep(h)]
        if q == NQ - 1:
            for dy in (2, 1, 3, 0):
                start(mine, mine, ws.at[q], wr.at[q, h], partner(h, dy))
        for dy in (2, 1, 3):
            start(mine, mine, us.at[q], ur.at[q, h], dev(0, dy, 0, 0))

    def gather_pair(q, h):
        wait(yrecv.at[q, h], ur.at[q, h])
        mine = lall.at[q, :, keep(h)]
        start(mine, mine, ws.at[q], wr.at[q, h], partner(h))

    load_b.wait()
    term(0)
    pl.semaphore_wait(barrier, len(near))
    for dz in (2, 14):
        signal(known.at[0], dev(dz, 0, 0, 0))
    send_pair(0)
    for q in range(1, NQ):
        term(q)
        send_pair(q)
        if q == 2:
            pl.semaphore_wait(known.at[0], 2)
            for dz in (4, 12):
                signal(known.at[1], dev(dz, 0, 0, 0))
    for u in range(len(units) + LATE):
        if u < len(units):
            send_y(*units[u])
        if u == LATE:
            pl.semaphore_wait(known.at[1], 2)
        if u >= LATE:
            send_z(*units[u - LATE])
    for u in units:
        finish_tile(*u)
    half, chunk = spart.shape[1] // NC, spart.shape[1] // (NC * NX)
    other = lax.rem(c + 1, NC)

    def score_term(q, halves):
        for h in halves:
            if q == NQ - 1:
                wait(yrecv.at[q, h], ur.at[q, h])
            wait(precv.at[q, h], wr.at[q, h])
        lo, hi = 128 * halves[0], 128 * (halves[-1] + 1)
        part = jnp.concatenate([lall[q, i, lo:hi] for i in range(NY)], axis=1)
        if q == NQ - 1:
            h, = halves
            for core in (other, c):
                spart[h, rows(core, half)] += dot(gbuf[q, rows(core, half)], part, ((1,), (1,)))
                if core is other:
                    start(spart.at[h, rows(other, half)], crecv.at[h], cs.at[h], cr.at[h], dev(0, 0, 0, 1))
            return
        t = dot(gbuf[q], part, ((1,), (1,)))
        for i, h in enumerate(halves):
            if q == 0:
                spart[h] = t[:, i * 128:(i + 1) * 128]
            else:
                spart[h] += t[:, i * 128:(i + 1) * 128]

    queue = [u for u in units if u[0] != NQ - 1]
    for i, u in enumerate(units):
        gather_y(*u)
        if i >= LATE and queue:
            gather_pair(*queue.pop(0))
    for u in queue:
        gather_pair(*u)
    score_term(0, (0, 1))
    score_term(1, (0, 1))
    score_term(2, (0,))
    score_term(3, (0,))
    score_term(2, (1,))
    score_term(3, (1,))
    for h in range(2):
        wait(crecv.at[h], cr.at[h])
        crecv[h] = crecv[h] + spart[h, rows(c, half)]
        xsend[h] = encode_wide(crecv[h])
        for dx in (2, 1, 3):
            to = lax.rem(x + dx, NX)
            start(xsend.at[h, rows(to, chunk)], xrecv.at[h, dx - 1], xs.at[h], xr.at[h], dev(0, 0, dx, 0))
    mine = c * NX + x
    r = []
    for h in range(2):
        wait(xrecv.at[h], xr.at[h])
        s = crecv[h, rows(x, chunk)]
        for i in range(NX - 1):
            s = s + decode_wide(xrecv[h, i])
        r.append(s * scale)
        sall[rows(mine, chunk), h * 128:(h + 1) * 128] = r[h]
        for i in range(h + 1):
            gp[i * 128:(i + 1) * 128, h * 128:(h + 1) * 128] = (
                dot(r[i], r[h], ((0,), (0,)), precision=lax.Precision.HIGHEST) * (1.0 / total)
            )

    def each_core(core, body):
        @pl.when(core == 0)
        def _():
            body(slice(None))

        @pl.when(core == 1)
        def _():
            body(pl.ds(128, 128))

    spot = (c * NX + x) * NY + y
    for core in range(NC):
        @pl.when(c == core)
        def _():
            for i, (dy, dx, dc) in enumerate(plane):
                lanes = pl.ds(128, 128) if (core + dc) % NC else slice(None)
                to = ((core + dc) % NC * NX + lax.rem(x + dx, NX)) * NY + lax.rem(y + dy, NY)
                start(
                    gp.at[rows(to, 8), lanes], gprecv.at[i, :, lanes],
                    ps.at[2], pr.at[2], dev(0, dy, dx, dc),
                )

    def sum_plane(lanes):
        wait(gprecv.at[:, :, lanes], pr.at[2])
        s = gp[rows(spot, 8), lanes]
        for i in range(len(plane)):
            s = s + gprecv[i, :, lanes]
        gzall[z, :, lanes] = s
        for dz in far:
            own = gzall.at[z, :, lanes]
            start(own, own, ps.at[6], pr.at[6], dev(dz, 0, 0, 0))

    each_core(c, sum_plane)
    for dx in (2, 1, 3):
        own = sall.at[rows(mine, chunk)]
        start(own, own, ps.at[4], pr.at[4], dev(0, 0, dx, 0))

    def sum_z(lanes):
        wait(gzall.at[pl.ds(0, NZ - 1), :, lanes], pr.at[6])
        s = gzall[0, :, lanes]
        for i in range(1, NZ):
            s = s + gzall[i, :, lanes]
        own = gram_ref.at[rows(spot, 8), lanes]
        own[...] = s
        for p in plane:
            start(own, own, ps.at[8], pr.at[8], dev(0, *p))

    for q in range(NQ):
        wait(psend.at[q], ks.at[q])
        wait(ysend.at[q], ys.at[q])
        wait(ysend.at[q], us.at[q])
        wait(psend.at[q], ws.at[q])

        @pl.when(lax.rem(pair + q, 2) == 0)
        def _():
            wait(lall.at[q, 0, pl.ds(0, 96)], zs.at[q])
            wait(zrecv.at[q], ls.at[q])

        @pl.when(lax.rem(pair + q, 2) == 1)
        def _():
            wait(lall.at[q, 0, pl.ds(0, 128)], zs.at[q])

    for h in range(2):
        wait(crecv.at[h], cs.at[h])
        wait(xrecv.at[h], xs.at[h])
    wait(sall.at[pl.ds(0, 3 * chunk)], pr.at[4])
    own = sall.at[rows(c, half)]
    start(own, own, ps.at[7], pr.at[7], dev(0, 0, 0, 1))
    out1 = pltpu.make_async_copy(own, scores_ref.at[rows(c, half)], out_sem.at[0])
    out1.start()
    each_core(c, sum_z)
    gram_ref[128:, :128] = jnp.zeros((128, 128), F32)
    wait(sall.at[pl.ds(0, half)], pr.at[7])
    own = sall.at[rows(other, half)]
    out2 = pltpu.make_async_copy(own, scores_ref.at[rows(other, half)], out_sem.at[1])
    out2.start()
    out1.wait()
    out2.wait()

    @pl.when(c == 0)
    def _():
        wait(spart.at[0, pl.ds(0, 368)], pr.at[8])

    @pl.when(c == 1)
    def _():
        wait(spart.at[0, pl.ds(0, 376)], pr.at[8])

    wait(sall.at[pl.ds(0, 3 * chunk)], ps.at[4])
    wait(sall.at[pl.ds(0, half)], ps.at[7])

    def sent(lanes):
        wait(gzall.at[pl.ds(0, NZ - 1), :, lanes], ps.at[6])
        wait(gprecv.at[:, :, lanes], ps.at[8])

    each_core(c, sent)

    @pl.when(c == 0)
    def _():
        wait(spart.at[0, pl.ds(0, 368)], ps.at[2])

    @pl.when(c == 1)
    def _():
        wait(spart.at[0, pl.ds(0, 376)], ps.at[2])


def scores_and_gram(genotypes, basis_in):
    n, v = genotypes.shape
    k = basis_in.shape[1]
    total_samples = n * lax.axis_size("samples")
    scale = 1.0 / (v * lax.axis_size("variants")) ** 0.5
    part = v // NQ
    chunk = n // (NC * NX)
    dma = pltpu.SemaphoreType.DMA
    vmem = pl.BlockSpec(memory_space=pltpu.VMEM)
    return pl.pallas_call(
        functools.partial(comm_kernel, scale, total_samples),
        out_shape=[jax.ShapeDtypeStruct((n, k), F32), jax.ShapeDtypeStruct((k, k), F32)],
        in_specs=[pl.BlockSpec(memory_space=pl.ANY)] * 2,
        out_specs=[pl.BlockSpec(memory_space=pl.ANY), vmem],
        scratch_shapes=[
            pltpu.VMEM((n, k), BF16),
            pltpu.VMEM((NQ, n, part), BF16),
            pltpu.VMEM((NQ, NY, k, 128), F32),
            pltpu.VMEM((NQ, 2, NY, k // 4, 128), BF16),
            pltpu.VMEM((NQ, 2, NY, k // 4, 128), BF16),
            pltpu.VMEM((NQ, 2, NY - 1, k // 4, 128), BF16),
            pltpu.VMEM((NQ, 2, NY - 1, k // 4, 128), BF16),
            pltpu.VMEM((NQ, 2, k // 4, 128), F32),
            pltpu.VMEM((NQ, 2, k // 4, 128), BF16),
            pltpu.VMEM((NQ, 2, 7 * 16, 128), BF16),
            pltpu.VMEM((NQ, NY, k, 128), BF16),
            pltpu.VMEM((2, n, k // 2), F32),
            pltpu.VMEM((2, n // NC, k // 2), F32),
            pltpu.VMEM((2, n // NC, k // 2), BF16),
            pltpu.VMEM((2, NX - 1, chunk, k // 2), BF16),
            pltpu.VMEM((n, k), F32),
            pltpu.VMEM((k, k), F32),
            pltpu.VMEM((NX * NY * NC - 1, 8, k), F32),
            pltpu.VMEM((NZ, 8, k), F32),
            dma((NQ + 1,)), dma((2,)), pltpu.SemaphoreType.REGULAR((2,)),
            dma((NQ,)), dma((NQ, 2, NY)), dma((NQ,)), dma((NQ, 2)), dma((NQ,)), dma((NQ, 2)),
            dma((NQ,)), dma((NQ, 2)), dma((NQ,)), dma((NQ, 2)), dma((NQ,)), dma((NQ, 2)),
            dma((2,)), dma((2,)), dma((2,)), dma((2,)),
            dma((9,)), dma((9,)),
        ],
        compiler_params=pltpu.CompilerParams(
            collective_id=0, has_side_effects=True, vmem_limit_bytes=24 << 20
        ),
        cost_estimate=pl.CostEstimate(flops=4 * n * v * k, bytes_accessed=2 * n * v, transcendentals=0),
        name="scores_and_gram",
    )(*(pltpu.with_memory_space_constraint(a, pltpu.HBM) for a in (genotypes, basis_in)))


def eliminate(a, panel):
    n = a.shape[0]
    row, col = (lax.broadcasted_iota(jnp.int32, (n, n), i) for i in (0, 1))
    eye = jnp.where(row == col, 1.0, 0.0)
    sub = lax.broadcasted_iota(jnp.int32, (8, n), 0)
    left = [a[8 * i:8 * i + 8] for i in range(n // 8)]
    right = [eye[8 * i:8 * i + 8] for i in range(n // 8)]
    upper, inverse = [], []
    for j0 in range(0, n, panel):
        lo = j0 // 8
        cols = [
            [jnp.broadcast_to(g[:, j0 + k:j0 + k + 1], (8, n)) for g in left[lo:]]
            for k in range(panel)
        ]
        for k in range(panel):
            j = j0 + k
            v, s = j // 8, j % 8
            pivot = cols[k][v - lo][s:s + 1]
            inv = 1.0 / pivot
            root = lax.rsqrt(pivot)
            ra, rb = left[v][s:s + 1], right[v][s:s + 1]
            upper.append(ra * root)
            inverse.append(rb * root)
            if j == n - 1:
                break
            sa = jnp.broadcast_to(ra * inv, (8, n))
            sb = jnp.broadcast_to(rb * inv, (8, n))
            sc = [jnp.broadcast_to(cols[m][v - lo][s:s + 1] * inv, (8, n)) for m in range(k + 1, panel)]
            for i in range(v if s < 7 else v + 1, n // 8):
                c = cols[k][i - lo]
                if i == v:
                    c = jnp.where(sub > s, c, 0.0)
                left[i] = left[i] - c * sa
                right[i] = right[i] - c * sb
                for m in range(k + 1, panel):
                    cols[m][i - lo] = cols[m][i - lo] - c * sc[m - k - 1]
    upper = jnp.where(row <= col, jnp.concatenate(upper, axis=0), 0.0)
    inverse = jnp.where(row >= col, jnp.concatenate(inverse, axis=0), 0.0)
    return upper, inverse


def split(a):
    high = a.astype(BF16)
    return high, (a - high.astype(F32)).astype(BF16)


def dot3(a, b, dims):
    (ah, al), (bh, bl) = split(a), split(b)
    return dot(ah, bh, dims) + (dot(ah, bl, dims) + dot(al, bh, dims))


def factor_kernel(panel, gram, scores_hbm, basis_hbm, factor_hbm, scores, basis, factor, sems):
    n = gram.shape[0]
    h = n // 2
    load = pltpu.make_async_copy(scores_hbm, scores, sems.at[0])
    load.start()
    u11, v1 = eliminate(gram[:h, :h], panel)
    load.wait()
    u12 = dot(v1, gram[:h, h:], ((1,), (0,)), precision=lax.Precision.HIGHEST)
    a22 = gram[h:, h:] - dot(u12, u12, ((0,), (0,)), precision=lax.Precision.HIGHEST)
    first = dot3(scores[:, :h], v1, ((1,), (1,)))
    rest = scores[:, h:] - dot3(first, u12, ((1,), (0,)))
    factor[:h, :h] = u11
    factor[:h, h:] = u12
    factor[h:, :h] = jnp.zeros((h, h), F32)
    basis[0] = first
    u22, v2 = eliminate(a22, panel)
    factor[h:, h:] = u22
    outs = [
        pltpu.make_async_copy(factor, factor_hbm, sems.at[3]),
        pltpu.make_async_copy(basis.at[0], basis_hbm.at[:, pl.ds(0, h)], sems.at[1]),
        pltpu.make_async_copy(basis.at[1], basis_hbm.at[:, pl.ds(h, h)], sems.at[2]),
    ]
    outs[0].start()
    outs[1].start()
    basis[1] = dot3(rest, v2, ((1,), (1,)))
    outs[2].start()
    for out in outs:
        out.wait()


def factor_and_basis(gram, scores):
    n, k = scores.shape
    vmem, hbm = pl.BlockSpec(memory_space=pltpu.VMEM), pl.BlockSpec(memory_space=pltpu.HBM)
    return pl.pallas_call(
        functools.partial(factor_kernel, 8),
        out_shape=[jax.ShapeDtypeStruct(scores.shape, F32), jax.ShapeDtypeStruct(gram.shape, F32)],
        in_specs=[vmem, hbm],
        out_specs=[hbm, hbm],
        scratch_shapes=[
            pltpu.VMEM((n, k), F32),
            pltpu.VMEM((2, n, k // 2), F32),
            pltpu.VMEM((k, k), F32),
            pltpu.SemaphoreType.DMA((4,)),
        ],
        compiler_params=pltpu.CompilerParams(vmem_limit_bytes=40 << 20),
        name="factor_and_basis",
    )(gram, scores)


def local(genotypes, basis_in):
    scores, gram = scores_and_gram(genotypes, basis_in)
    return tuple(factor_and_basis(gram, scores))


def solution(mesh):
    placed = (P("samples", "variants"), P("samples", None))
    return jax.shard_map(
        local, mesh=mesh, in_specs=placed, out_specs=(P("samples", None), P()), check_vma=False
    )
```
